256 devices in a mesh: ctx: 8 (over z), head: 4 (over x_hi, core), dp: 8 (over x_lo, y).
Axes of the slice: x: 4 (x_hi: 2, x_lo: 2; x = x_hi * 2 + x_lo), y: 4, z: 8, core: 2. Of those that a mesh axis runs over, the one named last changes fastest.
Arguments:
- query: bfloat16 [22528, 5120], P(('ctx', 'dp'), 'head'), may hold values from -4 to 4
- keys: bfloat16 [22528, 1024], P(('ctx', 'dp'), 'head'), may hold values from -4 to 4
- values: bfloat16 [22528, 1024], P(('ctx', 'dp'), 'head'), may hold values from -4 to 4
- output: bfloat16 [22528, 5120], P(('ctx', 'dp'), 'head'), may hold values from -3 to 3
- grad_out: bfloat16 [22528, 5120], P(('ctx', 'dp'), 'head'), may hold values from -4 to 4
- log_norm: bfloat16 [22528, 40], P(('ctx', 'dp'), 'head'), may hold values from 4 to 7
- route_counts: int32 [64, 64], replicated, may hold values from 0 to 11, as said below
- doc_lengths: int32 [8, 4], P('dp'), may hold values from 1 to 1408, 2816 in all within a row
Outputs:
- grad_query: bfloat16 [22528, 5120], P(('ctx', 'dp'), 'head')
- grad_key: bfloat16 [22528, 1024], P(('ctx', 'dp'), 'head')
- grad_value: bfloat16 [22528, 1024], P(('ctx', 'dp'), 'head')
The draws below stay inside these ranges and needn't reach their ends.
Inputs may be any that keep to these rules, and one draw needn't show every extreme that they name: Every row and every column of route_counts sums to 352; some entries equal 11 in every draw.
All inputs are finite; a program needn't handle non-finite values.
Results may differ from the reference program's by a relative error of at most 0.0051.
Values may be sent and summed in bfloat16 or wider, within the bound.
A program may use at most 192 MiB of HBM per device.

```python
import math
import jax
import jax.numpy as jnp
import numpy as np
from jax import lax

HEADS = 40
KV_HEADS = 8
HDIM = 128
TOK_DEV = 352
NDOC = 4
CONTEXT = 2816
ROWS = 22528
N_CTX = 8
N_DP = 8


def draw_route_counts(key, part):
    key = jax.random.fold_in(key, 11)
    owners = N_CTX * N_DP
    capacity = 2 * TOK_DEV // owners
    key_low, key_rows, key_cols = jax.random.split(key, 3)
    halves_low = jax.random.randint(key_low, (owners // 2,), 0, capacity + 1)
    halves_low = halves_low.at[0].set(capacity)
    pair_loads = jnp.stack([halves_low, capacity - halves_low], axis=1).reshape(owners)
    row_order = jax.random.permutation(key_rows, owners)
    col_order = jax.random.permutation(key_cols, owners)
    return pair_loads[(row_order[:, None] + col_order[None, :]) % owners].astype(jnp.int32)


def shard_levels(rng, shape, shards, low, top_value):
    gain = 1.0
    for position, parts in shards:
        steps = jax.random.uniform(jax.random.fold_in(jax.random.fold_in(rng, 6), position), (parts,), jnp.float32, low / len(shards), top_value / len(shards))
        gain = gain * jnp.repeat(jnp.exp(steps), shape[position] // parts).reshape((-1,) + (1,) * (len(shape) - 1 - position))
    return gain


def length_profile(number_of, total, limit, slope):
    loads = [(1 << 20) // math.isqrt(standing ** slope) + 1 for standing in range(2, number_of + 1)]
    rest, given = total - limit - (number_of - 1), [1] * (number_of - 1)
    while rest > 0:
        free = [i for i in range(number_of - 1) if given[i] < limit]
        mass, left = sum([loads[i] for i in free]), rest
        for i in free:
            extra = min(limit - given[i], max(1, left * loads[i] // mass), rest)
            given[i] = given[i] + extra
            rest = rest - extra
    return np.array([limit] + given)


def uneven(own_key, number_of, total, reach, skew):
    if number_of == 2:
        one = jax.random.randint(own_key, (), max(1, total - reach), min(reach, total - 1) + 1)
        return jnp.stack([one, total - one])
    tallies = jnp.asarray(length_profile(number_of, total, reach, skew), jnp.int32)
    twos = (number_of - 1) // 2
    source_of, receiver = tallies[1:1 + 2 * twos:2], tallies[2:2 + 2 * twos:2]
    room = jnp.minimum(source_of - 1, reach - receiver)
    passed = jax.random.randint(jax.random.fold_in(own_key, 1), (twos,), 0, 1 << 20) % (room + 1)
    tallies = tallies.at[1:1 + 2 * twos:2].set(source_of - passed).at[2:2 + 2 * twos:2].set(receiver + passed)
    return tallies[jax.random.permutation(jax.random.fold_in(own_key, 2), number_of)]


def noise(rng, dims, scale, limit, cuts=(), kind=jnp.bfloat16):
    factor_of = shard_levels(rng, dims, cuts, -0.22, 0.18) if cuts else 1.0
    array = jax.random.normal(rng, dims, jnp.float32) * scale * factor_of
    return jnp.minimum(jnp.maximum(array, -limit), limit).astype(kind)


def setup_inputs(seed: int = 0) -> dict:
    arg_keys = jax.random.split(jax.random.key(seed), 9)
    query = noise(arg_keys[0], (ROWS, HEADS * HDIM), 1.0, 4.0, ((0, 64), (1, 4)))
    keys = noise(arg_keys[1], (ROWS, KV_HEADS * HDIM), 1.0, 4.0, ((0, 64), (1, 4)))
    values = noise(arg_keys[2], (ROWS, KV_HEADS * HDIM), 1.0, 4.0, ((0, 64), (1, 4)))
    output = noise(arg_keys[3], (ROWS, HEADS * HDIM), 0.5, 3.0, ((0, 64), (1, 4)))
    grad_out = noise(arg_keys[4], (ROWS, HEADS * HDIM), 1.0, 4.0, ((0, 64), (1, 4)))
    log_norm = jnp.clip(4.0 + 3.0 * jax.random.uniform(arg_keys[5], (ROWS, HEADS), jnp.float32) ** shard_levels(arg_keys[5], (ROWS, HEADS), ((0, 64), (1, 4)), -0.2, 0.2), 4.0, 7.0).astype(jnp.bfloat16)
    route_counts = draw_route_counts(jax.random.fold_in(arg_keys[8], 71), 0)
    doc_lengths = jax.vmap(lambda own: uneven(own, NDOC, CONTEXT, CONTEXT // 2, 2))(jax.random.split(arg_keys[7], N_DP)).reshape((N_DP, NDOC)).astype(jnp.int32)
    return {"query": query, "keys": keys, "values": values, "output": output, "grad_out": grad_out, "log_norm": log_norm, "route_counts": route_counts, "doc_lengths": doc_lengths}


def context_sources(route_counts):
    send_starts = jnp.cumsum(route_counts, axis=1) - route_counts
    recv_ends = jnp.cumsum(route_counts, axis=0)
    recv_starts = recv_ends - route_counts
    row_ids = jnp.arange(TOK_DEV, dtype=jnp.int32)
    source = jnp.sum((recv_ends.T[:, None, :] <= row_ids[None, :, None]).astype(jnp.int32), axis=2).astype(jnp.int32)
    offset = row_ids[None, :] - jnp.take_along_axis(recv_starts.T, source, axis=1)
    sent_at = jnp.take_along_axis(send_starts.T, source, axis=1)
    rollout = (source * TOK_DEV + sent_at + offset).astype(jnp.int32)
    return rollout.reshape(N_CTX, N_DP, TOK_DEV).transpose(1, 0, 2).reshape(N_DP, N_CTX * TOK_DEV)


def group_grads(queries, key_rows, value_rows, grad_rows, delta, log_norm, visible):
    scale = HDIM ** -0.5
    scores = jnp.einsum("qrd,kd->rqk", queries, key_rows) * scale
    probs = jnp.where(visible[None], jnp.exp(scores - log_norm.T[:, :, None]), 0.0)
    probs_low = lax.optimization_barrier(probs.astype(jnp.bfloat16)).astype(jnp.float32)
    dvalues = jnp.einsum("rqk,qrd->kd", probs_low, grad_rows)
    dprob = jnp.einsum("qrd,kd->rqk", grad_rows, value_rows)
    dscore = (probs * (dprob - delta.T[:, :, None]) * scale).astype(jnp.bfloat16)
    dscore = lax.optimization_barrier(dscore).astype(jnp.float32)
    dquery = jnp.einsum("rqk,kd->qrd", dscore, key_rows)
    dkeys = jnp.einsum("rqk,qrd->kd", dscore, queries)
    return dquery, dkeys, dvalues


def reference(query, keys, values, output, grad_out, log_norm, route_counts, doc_lengths):
    group = HEADS // KV_HEADS
    length = N_CTX * TOK_DEV
    sources = context_sources(route_counts)
    positions = jnp.arange(length, dtype=jnp.int32)

    def one_context(item):
        rows, lengths_row = item
        bounds = jnp.cumsum(lengths_row)
        docs = jnp.sum((bounds[None, :] <= positions[:, None]).astype(jnp.int32), axis=1)
        visible = (positions[None, :] <= positions[:, None]) & (docs[None, :] == docs[:, None])
        q_ctx = query[rows].astype(jnp.float32).reshape(length, KV_HEADS, group, HDIM)
        do_ctx = grad_out[rows].astype(jnp.float32).reshape(length, KV_HEADS, group, HDIM)
        o_ctx = output[rows].astype(jnp.float32).reshape(length, KV_HEADS, group, HDIM)
        delta = lax.optimization_barrier(jnp.sum(do_ctx * o_ctx, axis=3).astype(jnp.bfloat16)).astype(jnp.float32)
        lse_ctx = log_norm[rows].astype(jnp.float32).reshape(length, KV_HEADS, group)
        k_ctx = keys[rows].astype(jnp.float32).reshape(length, KV_HEADS, HDIM)
        v_ctx = values[rows].astype(jnp.float32).reshape(length, KV_HEADS, HDIM)

        def one_group(index):
            return group_grads(q_ctx[:, index], k_ctx[:, index], v_ctx[:, index], do_ctx[:, index], delta[:, index], lse_ctx[:, index], visible)

        dquery, dkeys, dvalues = lax.map(one_group, jnp.arange(KV_HEADS, dtype=jnp.int32))
        dquery = dquery.transpose(1, 0, 2, 3).reshape(length, HEADS * HDIM)
        dkeys = dkeys.transpose(1, 0, 2).reshape(length, KV_HEADS * HDIM)
        dvalues = dvalues.transpose(1, 0, 2).reshape(length, KV_HEADS * HDIM)
        return dquery.astype(jnp.bfloat16), dkeys.astype(jnp.bfloat16), dvalues.astype(jnp.bfloat16)

    dquery, dkeys, dvalues = lax.map(one_context, (sources, doc_lengths))
    placed = sources.reshape(-1)
    grad_query = jnp.zeros((ROWS, HEADS * HDIM), jnp.bfloat16).at[placed].set(dquery.reshape(-1, HEADS * HDIM))
    grad_key = jnp.zeros((ROWS, KV_HEADS * HDIM), jnp.bfloat16).at[placed].set(dkeys.reshape(-1, KV_HEADS * HDIM))
    grad_value = jnp.zeros((ROWS, KV_HEADS * HDIM), jnp.bfloat16).at[placed].set(dvalues.reshape(-1, KV_HEADS * HDIM))
    return (grad_query, grad_key, grad_value)
```

```python
import functools

import jax
import jax.numpy as jnp
from jax import lax
from jax.experimental import pallas as pl
from jax.experimental.pallas import tpu as pltpu
from jax.sharding import PartitionSpec as P

HDIM = 128
NZ = 8
ND = 8
PAIR = 88
SLOTS = ND * PAIR
QB = 128
FAST = 448
SLOW = 704
FAR = 1 << 20
LOG2E = 1.4426950408889634
MESH = pl.DeviceIdType.MESH
BF = jnp.bfloat16
F32 = jnp.float32
VMEM_SPEC = pl.BlockSpec(memory_space=pltpu.VMEM)
SMEM_SPEC = pl.BlockSpec(memory_space=pltpu.SMEM)
ANY_SPEC = pl.BlockSpec(memory_space=pl.ANY)


def dot(a, b):
    return jnp.dot(a, b, preferred_element_type=F32)


def one_hot_rows(count, row):
    ids = lax.broadcasted_iota(jnp.int32, (count, row.shape[1]), 0)
    return jnp.where(ids == row, 1.0, 0.0).astype(BF)


def one_hot_cols(col, count):
    ids = lax.broadcasted_iota(jnp.int32, (col.shape[0], count), 1)
    return jnp.where(ids == col, 1.0, 0.0).astype(BF)


def ends_of(x, axis):
    n = x.shape[axis]
    x = jnp.moveaxis(x, axis, -1)
    tri = jnp.arange(n)[:, None] >= jnp.arange(n)[None, :]
    out = jnp.sum(jnp.where(tri, x[..., None, :], 0), axis=-1)
    return jnp.moveaxis(out, -1, axis)


def steps_to(ids, ends, base):
    jump = base[..., 1:] - base[..., :-1]
    past = ends[..., None, :-1] <= ids[:, None]
    return ids + base[..., :1] + jnp.sum(jnp.where(past, jump[..., None, :], 0), axis=-1)


def source_slots(rc, tok):
    rank = lax.axis_index(("ctx", "dp"))
    flat = lax.dynamic_index_in_dim(rc, rank, 0, keepdims=False)
    n = flat.reshape(NZ, ND)
    ends = ends_of(flat, 0)
    within = ends_of(n, 0) - n + jnp.arange(ND, dtype=jnp.int32)[None, :] * PAIR
    base = within.reshape(-1) - (ends - flat)
    return steps_to(jnp.arange(tok, dtype=jnp.int32), ends, base)


def plane_counts(rc):
    d = lax.axis_index("dp")
    return lax.dynamic_index_in_dim(rc.reshape(NZ * ND, NZ, ND), d, 2, keepdims=False).reshape(NZ, ND, NZ)


def compact_index(q):
    c0 = lax.axis_index("ctx")
    m = lax.dynamic_index_in_dim(q, c0, 0, keepdims=False)
    rows_end = ends_of(m, 1)
    mt = m.T.reshape(-1)
    cs = (ends_of(mt, 0) - mt).reshape(NZ, ND).T
    ids = jnp.arange(PAIR, dtype=jnp.int32)
    idx = steps_to(ids, rows_end, cs - (rows_end - m))
    return jnp.where(ids[None, :] < rows_end[:, -1:], idx, -1).reshape(-1)


def positions(q, cap, tok):
    load = jnp.sum(q, axis=1)
    chunk = jnp.arange(NZ, dtype=jnp.int32)[None, :] * tok
    ends = ends_of(load, 1)
    base = chunk + (ends_of(load, 0) - load) - (ends - load)
    ids = jnp.arange(cap, dtype=jnp.int32)
    pos = steps_to(ids, ends, base)
    return jnp.where(ids[None, :] < ends[:, -1:], pos, FAR)


def pack_kernel(q_ref, k_ref, v_ref, o_ref, g_ref, l_ref, slot_ref, kv_ref, qg_ref, stat):
    tok, width = q_ref.shape
    heads = width // HDIM
    kvw = k_ref.shape[1]
    pick = one_hot_rows(SLOTS, slot_ref[...])
    kv_ref[:, :kvw] = dot(pick, k_ref[...]).astype(BF)
    kv_ref[:, kvw:] = dot(pick, v_ref[...]).astype(BF)
    stat[...] = jnp.zeros_like(stat)
    stat[:, :heads] = l_ref[...].astype(F32)
    for h in range(heads):
        at = slice(h * HDIM, (h + 1) * HDIM)
        both = g_ref[:, at].astype(F32) * o_ref[:, at].astype(F32)
        stat[:, heads + h:heads + h + 1] = jnp.sum(both, axis=1, keepdims=True)
    for h in range(0, heads, 2):
        at = slice(h * HDIM, (h + 2) * HDIM)
        qg_ref[:, at] = dot(pick, q_ref[:, at]).astype(BF)
        to = slice(width + h * HDIM, width + (h + 2) * HDIM)
        qg_ref[:, to] = dot(pick, g_ref[:, at]).astype(BF)
    qg_ref[:, 2 * width:] = dot(pick, stat[...].astype(BF)).astype(BF)


def pack(query, keys, values, output, grad_out, log_norm, slot_row):
    tok, width = query.shape
    kvw = 2 * keys.shape[1]
    qgw = 2 * width + HDIM
    return pl.pallas_call(
        pack_kernel,
        out_shape=(
            jax.ShapeDtypeStruct((SLOTS, kvw), BF),
            jax.ShapeDtypeStruct((SLOTS, qgw), BF),
        ),
        in_specs=[VMEM_SPEC] * 7,
        out_specs=(VMEM_SPEC, VMEM_SPEC),
        scratch_shapes=[pltpu.VMEM((tok, HDIM), F32)],
        compiler_params=pltpu.CompilerParams(vmem_limit_bytes=40 << 20),
        name="pack_rows",
    )(query, keys, values, output, grad_out, log_norm, slot_row)


def greet():
    z = lax.axis_index("ctx")
    d = lax.axis_index("dp")
    barrier = pltpu.get_barrier_semaphore()
    for s in range(1, ND):
        pl.semaphore_signal(barrier, inc=1, device_id={"dp": lax.rem(d + s, ND)}, device_id_type=MESH)
    for s in (1, NZ - 1):
        pl.semaphore_signal(barrier, inc=1, device_id={"ctx": lax.rem(z + s, NZ)}, device_id_type=MESH)
    pl.semaphore_wait(barrier, ND + 1)


def exchange(src, dst, send, recv):
    d = lax.axis_index("dp")
    copies = []
    for s in range(1, ND):
        to = lax.rem(d + s, ND)
        copies.append(pltpu.make_async_remote_copy(
            src_ref=src.at[to], dst_ref=dst.at[d], send_sem=send.at[s], recv_sem=recv.at[s],
            device_id={"dp": to}, device_id_type=MESH))
    return copies


def along(axis_by, src, dst, send, recv):
    z = lax.axis_index("ctx")
    return pltpu.make_async_remote_copy(
        src_ref=src, dst_ref=dst, send_sem=send, recv_sem=recv,
        device_id={"ctx": lax.rem(z + axis_by, NZ)}, device_id_type=MESH)


def dispatch_kernel(kv_ref, qg_ref, idx_ref, all_ref, rqg_ref, rkv, mine,
                    ks, kr, qs, qr, ls, fs, fr, bs, br):
    z = lax.axis_index("ctx")
    d = lax.axis_index("dp")
    cap = mine.shape[0]
    part = cap // 2
    greet()
    kv_copies = exchange(kv_ref, rkv, ks, kr)
    for c in kv_copies:
        c.start()
    own = pltpu.make_async_copy(kv_ref.at[d], rkv.at[d], ls.at[0])
    own.start()
    own.wait()
    for c in kv_copies:
        c.wait_recv()
    pick = one_hot_rows(cap, idx_ref[...])
    mine[...] = dot(pick, rkv[...].reshape(SLOTS, rkv.shape[2])).astype(BF)
    keep = pltpu.make_async_copy(mine, all_ref.at[z], ls.at[1])
    sent = []

    def hop(step, piece):
        rows = pl.ds(piece * part, part)
        for by, origin, send, recv, half in (
                (1, lax.rem(z - step + NZ, NZ), fs, fr, 0), (NZ - 1, lax.rem(z + step, NZ), bs, br, 1)):
            if step == NZ // 2 - 1 and piece != half:
                continue
            src = mine.at[rows] if step == 0 else all_ref.at[origin, rows]
            c = along(by, src, all_ref.at[origin, rows], send.at[step, piece], recv.at[step, piece])
            c.start()
            sent.append((step, piece, c))

    for piece in range(2):
        hop(0, piece)
    keep.start()
    qg_copies = exchange(qg_ref, rqg_ref, qs, qr)
    for c in qg_copies:
        c.start()
    own = pltpu.make_async_copy(qg_ref.at[d], rqg_ref.at[d], ls.at[2])
    own.start()
    for step in range(1, NZ // 2):
        for piece in range(2):
            for s, p, c in list(sent):
                if s == step - 1 and p == piece:
                    c.wait_recv()
            hop(step, piece)
    for s, p, c in sent:
        if s == NZ // 2 - 1:
            c.wait_recv()
    for s, p, c in sent:
        c.wait_send()
    for c in kv_copies:
        c.wait_send()
    for c in qg_copies:
        c.wait()
    keep.wait()
    own.wait()


def dispatch(kv, qg, idx_row, cap, cid):
    kvw = kv.shape[1]
    qgw = qg.shape[1]
    dma = pltpu.SemaphoreType.DMA
    return pl.pallas_call(
        dispatch_kernel,
        out_shape=(
            jax.ShapeDtypeStruct((NZ, cap, kvw), BF),
            jax.ShapeDtypeStruct((ND, PAIR, qgw), BF),
        ),
        in_specs=[VMEM_SPEC, ANY_SPEC, VMEM_SPEC],
        out_specs=(ANY_SPEC, ANY_SPEC),
        scratch_shapes=[
            pltpu.VMEM((ND, PAIR, kvw), BF), pltpu.VMEM((cap, kvw), BF),
            dma((ND,)), dma((ND,)), dma((ND,)), dma((ND,)), dma((3,)),
            dma((4, 2)), dma((4, 2)), dma((4, 2)), dma((4, 2)),
        ],
        compiler_params=pltpu.CompilerParams(
            collective_id=cid, has_side_effects=True, vmem_limit_bytes=40 << 20),
        name="dispatch_rows",
    )(kv.reshape(ND, PAIR, kvw), qg.reshape(ND, PAIR, qgw), idx_row)


def attend_kernel(group, kvh, kb, flag_ref, all_ref, rqg_ref, row_ref, col_ref, kpos_ref, qpos_ref,
                  dkv_ref, dq_ref, qs, gs, lse, dlt, dq, dkv):
    nq = qs.shape[1]
    capq = nq * QB
    width = group * kvh * HDIM
    heads = group * kvh
    kvw = kvh * HDIM
    scale = HDIM ** -0.5
    tiles = all_ref.shape[0] // kb
    pick = one_hot_rows(capq, row_ref[...])
    stat = lax.dot_general(rqg_ref[:, 2 * width:], pick, (((0,), (1,)), ((), ())), preferred_element_type=F32)
    for h in range(heads):
        g, r = divmod(h, group)
        for src, dst in ((0, qs), (width, gs)):
            part = dot(pick, rqg_ref[:, src + h * HDIM:src + (h + 1) * HDIM]).astype(BF)
            for i in range(nq):
                dst[g, i, r * QB:(r + 1) * QB, :] = part[i * QB:(i + 1) * QB, :]
        for i in range(nq):
            at = slice(i * QB, (i + 1) * QB)
            to = slice(r * QB, (r + 1) * QB)
            lse[g, i, :, to] = jnp.broadcast_to(stat[h:h + 1, at] * LOG2E, (8, QB))
            dlt[g, i, :, to] = jnp.broadcast_to(stat[heads + h:heads + h + 1, at], (8, QB))
    dq[...] = jnp.zeros_like(dq)
    dkv[...] = jnp.zeros_like(dkv)

    def q_block(i, _):
        hi = qpos_ref[i, 0:1, :]
        lo = qpos_ref[i, 1:2, :]

        def k_tile(t, _):
            @pl.when(flag_ref[i, t] != 0)
            def _():
                rows = pl.ds(pl.multiple_of(t * kb, 16), kb)
                kp = kpos_ref[rows, :]
                seen = (kp <= hi) & (kp >= lo)
                keep = jnp.where(seen, 1.0, 0.0)
                keep = jnp.concatenate([keep] * group, axis=1) > 0.5
                for g in range(kvh):
                    kt = all_ref[rows, g * HDIM:(g + 1) * HDIM]
                    vt = all_ref[rows, kvw + g * HDIM:kvw + (g + 1) * HDIM]
                    qt = qs[g, i]
                    gt = gs[g, i]
                    contract = (((1,), (1,)), ((), ()))
                    s = lax.dot_general(kt, qt, contract, preferred_element_type=F32)
                    p = jnp.where(keep, jnp.exp2(s * (scale * LOG2E) - lse[g, i, 0:1, :]), 0.0)
                    dp = lax.dot_general(vt, gt, contract, preferred_element_type=F32)
                    ds = (p * (dp - dlt[g, i, 0:1, :]) * scale).astype(BF)
                    dkv[rows, kvw + g * HDIM:kvw + (g + 1) * HDIM] += dot(p.astype(BF), gt)
                    dkv[rows, g * HDIM:(g + 1) * HDIM] += dot(ds, qt)
                    dq[g, i] += lax.dot_general(ds, kt, (((0,), (0,)), ((), ())), preferred_element_type=F32)
            return 0

        lax.fori_loop(0, tiles, k_tile, 0)
        return 0

    lax.fori_loop(0, nq, q_block, 0)
    dkv_ref[...] = dkv[...].astype(BF)
    back = one_hot_cols(col_ref[...], capq)
    for h in range(heads):
        g, r = divmod(h, group)
        rows = jnp.concatenate([dq[g, i, r * QB:(r + 1) * QB, :] for i in range(nq)], axis=0).astype(BF)
        dq_ref[:, h * HDIM:(h + 1) * HDIM] = dot(back, rows).astype(BF)


def attend(flags, kv_all, rqg, idx, kpos, qpos, group, kvh, kb):
    total, kvw = kv_all.shape
    nq = qpos.shape[0]
    width = group * kvh * HDIM
    return pl.pallas_call(
        functools.partial(attend_kernel, group, kvh, kb),
        out_shape=(
            jax.ShapeDtypeStruct((total, kvw), BF),
            jax.ShapeDtypeStruct((SLOTS, width), BF),
        ),
        in_specs=[SMEM_SPEC] + [VMEM_SPEC] * 6,
        out_specs=(VMEM_SPEC, VMEM_SPEC),
        scratch_shapes=[
            pltpu.VMEM((kvh, nq, group * QB, HDIM), BF), pltpu.VMEM((kvh, nq, group * QB, HDIM), BF),
            pltpu.VMEM((kvh, nq, 8, group * QB), F32), pltpu.VMEM((kvh, nq, 8, group * QB), F32),
            pltpu.VMEM((kvh, nq, group * QB, HDIM), F32), pltpu.VMEM((total, kvw), F32),
        ],
        compiler_params=pltpu.CompilerParams(vmem_limit_bytes=56 << 20),
        name="attention_grads",
    )(flags, kv_all, rqg, idx.reshape(1, -1), idx.reshape(-1, 1), kpos, qpos)


def return_kernel(dkv_ref, dq_ref, col_ref, rdq_ref, rdkv_ref, fin, bin_, fout, bout, slots,
                  qs, qr, ks, kr, ls, fs, fr, bs, br):
    z = lax.axis_index("ctx")
    d = lax.axis_index("dp")
    cap, kvw = dkv_ref.shape[1:]
    part = cap // 2
    last = NZ // 2 - 1
    greet()
    sent = []

    def hop(step, piece):
        rows = pl.ds(piece * part, part)
        for by, owner, send, recv, into, out, half in (
                (1, lax.rem(z + NZ // 2 - step, NZ), fs, fr, fin, fout, 0),
                (NZ - 1, lax.rem(z + NZ // 2 + step, NZ), bs, br, bin_, bout, 1)):
            if step == 0 and piece != half:
                continue
            if step == 0 or (step == 1 and piece != half):
                src = dkv_ref.at[owner, rows]
            else:
                for s, p, b, c in sent:
                    if s == step - 1 and p == piece and b == by:
                        c.wait_recv()
                out[step, rows, :] = (dkv_ref[owner, rows, :].astype(F32)
                                      + into[step - 1, rows, :].astype(F32)).astype(BF)
                src = out.at[step, rows]
            c = along(by, src, into.at[step, rows], send.at[step, piece], recv.at[step, piece])
            c.start()
            sent.append((step, piece, by, c))

    hop(0, 0)
    hop(0, 1)
    dq_copies = exchange(dq_ref, rdq_ref, qs, qr)
    for c in dq_copies:
        c.start()
    own = pltpu.make_async_copy(dq_ref.at[d], rdq_ref.at[d], ls.at[0])
    own.start()
    hop(1, 1)
    hop(1, 0)
    for step in range(2, NZ // 2):
        hop(step, 0)
        hop(step, 1)
    for s, p, b, c in sent:
        if s == last:
            c.wait_recv()
    total = (dkv_ref[z].astype(F32) + fin[last].astype(F32) + bin_[last].astype(F32)).astype(BF)
    back = one_hot_cols(col_ref[...], cap)
    slots[...] = dot(back, total).astype(BF).reshape(slots.shape)
    kv_copies = exchange(slots, rdkv_ref, ks, kr)
    for c in kv_copies:
        c.start()
    own_kv = pltpu.make_async_copy(slots.at[d], rdkv_ref.at[d], ls.at[1])
    own_kv.start()
    for s, p, b, c in sent:
        c.wait_send()
    own.wait()
    own_kv.wait()
    for c in dq_copies:
        c.wait()
    for c in kv_copies:
        c.wait()


def send_back(dkv, dq, idx, cid):
    total, kvw = dkv.shape
    cap = total // NZ
    width = dq.shape[1]
    dma = pltpu.SemaphoreType.DMA
    return pl.pallas_call(
        return_kernel,
        out_shape=(
            jax.ShapeDtypeStruct((ND, PAIR, width), BF),
            jax.ShapeDtypeStruct((ND, PAIR, kvw), BF),
        ),
        in_specs=[VMEM_SPEC, ANY_SPEC, VMEM_SPEC],
        out_specs=(ANY_SPEC, ANY_SPEC),
        scratch_shapes=[pltpu.VMEM((NZ // 2, cap, kvw), BF)] * 4 + [
            pltpu.VMEM((ND, PAIR, kvw), BF),
            dma((ND,)), dma((ND,)), dma((ND,)), dma((ND,)), dma((2,)),
            dma((4, 2)), dma((4, 2)), dma((4, 2)), dma((4, 2)),
        ],
        compiler_params=pltpu.CompilerParams(
            collective_id=cid, has_side_effects=True, vmem_limit_bytes=48 << 20),
        name="return_rows",
    )(dkv.reshape(NZ, cap, kvw), dq.reshape(ND, PAIR, width), idx.reshape(-1, 1))


def unpack_kernel(dq_ref, dkv_ref, slot_ref, gq_ref, gk_ref, gv_ref):
    width = dq_ref.shape[1]
    kvw = gk_ref.shape[1]
    pick = one_hot_cols(slot_ref[...], SLOTS)
    for at in range(0, width, 2 * HDIM):
        gq_ref[:, at:at + 2 * HDIM] = dot(pick, dq_ref[:, at:at + 2 * HDIM]).astype(BF)
    gk_ref[...] = dot(pick, dkv_ref[:, :kvw]).astype(BF)
    gv_ref[...] = dot(pick, dkv_ref[:, kvw:]).astype(BF)


def unpack(rdq, rdkv, slot_col):
    tok = slot_col.shape[0]
    width = rdq.shape[2]
    kvw = rdkv.shape[2] // 2
    return pl.pallas_call(
        unpack_kernel,
        out_shape=(
            jax.ShapeDtypeStruct((tok, width), BF),
            jax.ShapeDtypeStruct((tok, kvw), BF),
            jax.ShapeDtypeStruct((tok, kvw), BF),
        ),
        in_specs=[VMEM_SPEC] * 3,
        out_specs=(VMEM_SPEC,) * 3,
        compiler_params=pltpu.CompilerParams(vmem_limit_bytes=32 << 20),
        name="unpack_rows",
    )(rdq.reshape(SLOTS, width), rdkv.reshape(SLOTS, 2 * kvw), slot_col)


def body(query, keys, values, output, grad_out, log_norm, route_counts, doc_lengths):
    tok = query.shape[0]
    kvh = keys.shape[1] // HDIM
    group = query.shape[1] // keys.shape[1]
    slot = source_slots(route_counts, tok)
    q = plane_counts(route_counts)
    idx = compact_index(q)
    kv, qg = pack(query, keys, values, output, grad_out, log_norm, slot.reshape(1, -1))
    most = jnp.max(jnp.sum(route_counts.reshape(NZ, ND, NZ, ND), axis=(1, 2)))

    def run(cap, kb, cid, kv, qg):
        capq = -(-cap // QB) * QB
        pos = positions(q, cap, tok)
        mine = lax.dynamic_index_in_dim(pos, lax.axis_index("ctx"), 0, keepdims=False)
        mine = jnp.pad(mine, (0, capq - cap), constant_values=FAR)
        bounds = ends_of(doc_lengths[0], 0)
        lo = jnp.max(jnp.where(bounds[None, :] <= mine[:, None], bounds[None, :], 0), axis=1)
        hi = jnp.where(mine < FAR, mine, -1)
        qpos = jnp.stack([hi.reshape(-1, QB), lo.reshape(-1, QB)], axis=1)
        k_tiles = pos.reshape(-1, kb)
        k_min = jnp.min(k_tiles, axis=1)
        k_max = jnp.max(jnp.where(k_tiles < FAR, k_tiles, -1), axis=1)
        q_max = jnp.max(qpos[:, 0, :], axis=1)
        q_min = jnp.min(jnp.where(qpos[:, 0, :] >= 0, qpos[:, 1, :], FAR), axis=1)
        flags = ((k_min[None, :] <= q_max[:, None]) & (k_max[None, :] >= q_min[:, None])).astype(jnp.int32)
        kv_all, rqg = dispatch(kv, qg, idx.reshape(1, -1), cap, cid)
        dkv, dq = attend(flags, kv_all.reshape(NZ * cap, -1), rqg.reshape(SLOTS, -1), idx,
                         pos.reshape(-1, 1), qpos, group, kvh, kb)
        return send_back(dkv, dq, idx, cid + 1)

    rdq, rdkv = lax.cond(
        most <= FAST, functools.partial(run, FAST, 112, 0), functools.partial(run, SLOW, 176, 2), kv, qg)
    return unpack(rdq, rdkv, slot.reshape(-1, 1))


def solution(mesh):
    rows = P(("ctx", "dp"), "head")
    return jax.shard_map(
        body, mesh=mesh, in_specs=(rows,) * 6 + (P(), P("dp", None)), out_specs=(rows,) * 3, check_vma=False)
```

```python
import functools

import jax
import jax.numpy as jnp
from jax import lax
from jax.experimental import pallas as pl
from jax.experimental.pallas import tpu as pltpu
from jax.sharding import PartitionSpec as P

HDIM = 128
NZ = 8
ND = 8
QB = 128
KS = 32
FAST = (448, 80)
SLOW = (704, 88)
FAR = 1 << 20
LOG2E = 1.4426950408889634
MESH = pl.DeviceIdType.MESH
BF = jnp.bfloat16
F32 = jnp.float32
VMEM_SPEC = pl.BlockSpec(memory_space=pltpu.VMEM)
SMEM_SPEC = pl.BlockSpec(memory_space=pltpu.SMEM)
ANY_SPEC = pl.BlockSpec(memory_space=pl.ANY)


def dot(a, b):
    return jnp.dot(a, b, preferred_element_type=F32)


def one_hot_rows(count, row):
    ids = lax.broadcasted_iota(jnp.int32, (count, row.shape[1]), 0)
    return jnp.where(ids == row, 1.0, 0.0).astype(BF)


def dot_rows(a, b):
    return lax.dot_general(a, b, (((0,), (0,)), ((), ())), preferred_element_type=F32)


def ends_of(x, axis):
    n = x.shape[axis]
    x = jnp.moveaxis(x, axis, -1)
    tri = jnp.arange(n)[:, None] >= jnp.arange(n)[None, :]
    out = jnp.sum(jnp.where(tri, x[..., None, :], 0), axis=-1)
    return jnp.moveaxis(out, -1, axis)


def steps_to(ids, ends, base):
    jump = base[..., 1:] - base[..., :-1]
    past = ends[..., None, :-1] <= ids[:, None]
    return ids + base[..., :1] + jnp.sum(jnp.where(past, jump[..., None, :], 0), axis=-1)


def source_slots(rc, tok, pair):
    rank = lax.axis_index(("ctx", "dp"))
    flat = lax.dynamic_index_in_dim(rc, rank, 0, keepdims=False)
    n = flat.reshape(NZ, ND)
    ends = ends_of(flat, 0)
    within = ends_of(n, 0) - n + jnp.arange(ND, dtype=jnp.int32)[None, :] * pair
    base = within.reshape(-1) - (ends - flat)
    return steps_to(jnp.arange(tok, dtype=jnp.int32), ends, base)


def plane_counts(rc):
    d = lax.axis_index("dp")
    return lax.dynamic_index_in_dim(rc.reshape(NZ * ND, NZ, ND), d, 2, keepdims=False).reshape(NZ, ND, NZ)


def compact_index(q, pair):
    c0 = lax.axis_index("ctx")
    m = lax.dynamic_index_in_dim(q, c0, 0, keepdims=False)
    rows_end = ends_of(m, 1)
    mt = m.T.reshape(-1)
    cs = (ends_of(mt, 0) - mt).reshape(NZ, ND).T
    ids = jnp.arange(pair, dtype=jnp.int32)
    idx = steps_to(ids, rows_end, cs - (rows_end - m))
    return jnp.where(ids[None, :] < rows_end[:, -1:], idx, -1).reshape(-1)


def positions(q, cap, tok):
    load = jnp.sum(q, axis=1)
    chunk = jnp.arange(NZ, dtype=jnp.int32)[None, :] * tok
    ends = ends_of(load, 1)
    base = chunk + (ends_of(load, 0) - load) - (ends - load)
    ids = jnp.arange(cap, dtype=jnp.int32)
    pos = steps_to(ids, ends, base)
    return jnp.where(ids[None, :] < ends[:, -1:], pos, FAR), jnp.concatenate([ends, base], axis=1)


def greet():
    z = lax.axis_index("ctx")
    d = lax.axis_index("dp")
    barrier = pltpu.get_barrier_semaphore()
    for s in range(1, ND):
        pl.semaphore_signal(barrier, inc=1, device_id={"dp": lax.rem(d + s, ND)}, device_id_type=MESH)
    for s in (1, NZ - 1):
        pl.semaphore_signal(barrier, inc=1, device_id={"ctx": lax.rem(z + s, NZ)}, device_id_type=MESH)
    pl.semaphore_wait(barrier, ND + 1)


def exchange(src, dst, send, recv):
    d = lax.axis_index("dp")
    copies = []
    for s in range(1, ND):
        to = lax.rem(d + s, ND)
        copies.append(pltpu.make_async_remote_copy(
            src_ref=src.at[to], dst_ref=dst.at[d], send_sem=send.at[s], recv_sem=recv.at[s],
            device_id={"dp": to}, device_id_type=MESH))
    return copies


def along(axis_by, src, dst, send, recv):
    z = lax.axis_index("ctx")
    return pltpu.make_async_remote_copy(
        src_ref=src, dst_ref=dst, send_sem=send, recv_sem=recv,
        device_id={"ctx": lax.rem(z + axis_by, NZ)}, device_id_type=MESH)


def dispatch_kernel(q_ref, k_ref, v_ref, o_ref, g_ref, l_ref, slot_ref, idx_ref, all_ref, rq_ref, rg_ref,
                    qv, kvv, ov, gv, stat, skv, sq, sg, rkv, mine,
                    ins, ks, kr, qs, qr, gs, gr, ls, fs, fr, bs, br):
    z = lax.axis_index("ctx")
    d = lax.axis_index("dp")
    width = qv.shape[1]
    heads = width // HDIM
    kvw = k_ref.shape[1]
    slots, pair = skv.shape[0] * skv.shape[1], skv.shape[1]
    cap = mine.shape[0]
    part = cap // 2
    loads = []
    for n, (src, dst) in enumerate(((k_ref, kvv.at[:, :kvw]), (v_ref, kvv.at[:, kvw:]),
                                    (q_ref, qv), (g_ref, gv), (o_ref, ov))):
        c = pltpu.make_async_copy(src, dst, ins.at[n])
        c.start()
        loads.append(c)
    greet()
    pick = one_hot_rows(slots, slot_ref[...])
    loads[0].wait()
    loads[1].wait()
    skv[...] = dot(pick, kvv[...]).astype(BF).reshape(skv.shape)
    kv_copies = exchange(skv, rkv, ks, kr)
    for c in kv_copies:
        c.start()
    own = [pltpu.make_async_copy(skv.at[d], rkv.at[d], ls.at[0])]
    own[0].start()
    loads[2].wait()
    for at in range(0, width, 2 * HDIM):
        at = slice(at, at + 2 * HDIM)
        sq[:, :, at] = dot(pick, qv[:, at]).astype(BF).reshape(ND, pair, 2 * HDIM)
    q_copies = exchange(sq, rq_ref, qs, qr)
    for c in q_copies:
        c.start()
    own.append(pltpu.make_async_copy(sq.at[d], rq_ref.at[d], ls.at[1]))
    own[1].start()
    loads[3].wait()
    loads[4].wait()
    stat[...] = jnp.zeros_like(stat)
    for h in range(heads):
        at = slice(h * HDIM, (h + 1) * HDIM)
        both = gv[:, at].astype(F32) * ov[:, at].astype(F32)
        stat[:, h:h + 1] = jnp.sum(both, axis=1, keepdims=True)
    for at in range(0, width, 2 * HDIM):
        at = slice(at, at + 2 * HDIM)
        sg[:, :, at] = dot(pick, gv[:, at]).astype(BF).reshape(ND, pair, 2 * HDIM)
    sg[:, :, width:] = dot(pick, stat[...].astype(BF)).astype(BF).reshape(ND, pair, HDIM)
    lse = lax.dot_general(pick, l_ref[...], (((1,), (1,)), ((), ())), preferred_element_type=F32)
    sg[:, :, width + heads:width + 2 * heads] = lse.astype(BF).reshape(ND, pair, heads)
    g_copies = exchange(sg, rg_ref, gs, gr)
    for c in g_copies:
        c.start()
    own.append(pltpu.make_async_copy(sg.at[d], rg_ref.at[d], ls.at[2]))
    own[2].start()
    own[0].wait()
    for c in kv_copies:
        c.wait_recv()
    mine[...] = dot(one_hot_rows(cap, idx_ref[...]), rkv[...].reshape(slots, 2 * kvw)).astype(BF)
    sent = []

    def hop(step, piece):
        rows = pl.ds(piece * part, part)
        for by, origin, send, recv, half in (
                (1, lax.rem(z - step + NZ, NZ), fs, fr, 0), (NZ - 1, lax.rem(z + step, NZ), bs, br, 1)):
            if step == NZ // 2 - 1 and piece != half:
                continue
            src = mine.at[rows] if step == 0 else all_ref.at[origin, rows]
            c = along(by, src, all_ref.at[origin, rows], send.at[step, piece], recv.at[step, piece])
            c.start()
            sent.append((step, piece, c))

    for piece in range(2):
        hop(0, piece)
    own.append(pltpu.make_async_copy(mine, all_ref.at[z], ls.at[3]))
    own[3].start()
    for step in range(1, NZ // 2):
        for piece in range(2):
            for s, p, c in list(sent):
                if s == step - 1 and p == piece:
                    c.wait_recv()
            hop(step, piece)
    for s, p, c in sent:
        if s == NZ // 2 - 1:
            c.wait_recv()
        c.wait_send()
    for c in kv_copies:
        c.wait_send()
    for c in q_copies + g_copies:
        c.wait()
    for c in own[1:]:
        c.wait()


def dispatch(query, keys, values, output, grad_out, log_norm, slot_row, idx_row, cap, pair, cid):
    tok, width = query.shape
    kvw = 2 * keys.shape[1]
    gw = width + HDIM
    dma = pltpu.SemaphoreType.DMA
    return pl.pallas_call(
        dispatch_kernel,
        out_shape=(
            jax.ShapeDtypeStruct((NZ, cap, kvw), BF),
            jax.ShapeDtypeStruct((ND, pair, width), BF),
            jax.ShapeDtypeStruct((ND, pair, gw), BF),
        ),
        in_specs=[ANY_SPEC] * 5 + [VMEM_SPEC] * 3,
        out_specs=(ANY_SPEC,) * 3,
        scratch_shapes=[
            pltpu.VMEM((tok, width), BF), pltpu.VMEM((tok, kvw), BF),
            pltpu.VMEM((tok, width), BF), pltpu.VMEM((tok, width), BF), pltpu.VMEM((tok, HDIM), F32),
            pltpu.VMEM((ND, pair, kvw), BF), pltpu.VMEM((ND, pair, width), BF), pltpu.VMEM((ND, pair, gw), BF),
            pltpu.VMEM((ND, pair, kvw), BF), pltpu.VMEM((cap, kvw), BF),
            dma((5,)), dma((ND,)), dma((ND,)), dma((ND,)), dma((ND,)), dma((ND,)), dma((ND,)), dma((4,)),
            dma((4, 2)), dma((4, 2)), dma((4, 2)), dma((4, 2)),
        ],
        compiler_params=pltpu.CompilerParams(
            collective_id=cid, has_side_effects=True, vmem_limit_bytes=56 << 20),
        name="dispatch_rows",
    )(query, keys, values, output, grad_out, log_norm.T, slot_row, idx_row)


def attend_kernel(group, kvh, span_ref, tab_ref, all_hbm, rq_hbm, rg_hbm, row_ref, qpos_ref, dkv_ref, dq_ref,
                  all_ref, rq_ref, rg_ref, qs, gs, lse, dlt, dq, dkv, kpos, ins):
    nq = qs.shape[1]
    capq = nq * QB
    heads = group * kvh
    width = heads * HDIM
    kvw = kvh * HDIM
    scale = HDIM ** -0.5
    cap = all_ref.shape[1]
    tile = NZ * KS
    loads = []
    for n, (src, dst) in enumerate(((rq_hbm, rq_ref), (rg_hbm, rg_ref), (all_hbm, all_ref))):
        c = pltpu.make_async_copy(src, dst, ins.at[n])
        c.start()
        loads.append(c)
    pick = one_hot_rows(capq, row_ref[...])
    ids = lax.broadcasted_iota(jnp.int32, (cap, HDIM), 0)
    for z in range(NZ):
        p = ids + tab_ref[z, NZ]
        for c in range(NZ):
            jump = tab_ref[z, NZ + c + 1] - tab_ref[z, NZ + c] if c + 1 < NZ else FAR
            p = p + jnp.where(ids >= tab_ref[z, c], jump, 0)
        kpos[z] = p
    dq[...] = jnp.zeros_like(dq)
    dkv[...] = jnp.zeros_like(dkv)
    for load, src, dst in ((loads[0], rq_ref, qs), (loads[1], rg_ref, gs)):
        load.wait()
        for h in range(0, heads, 2):
            both = dot(pick, src[:, h * HDIM:(h + 2) * HDIM]).astype(BF)
            for e in range(2):
                g, r = divmod(h + e, group)
                for i in range(nq):
                    dst[g, i, r * QB:(r + 1) * QB, :] = both[i * QB:(i + 1) * QB, e * HDIM:(e + 1) * HDIM]
    stat = lax.dot_general(rg_ref[:, width:], pick, (((0,), (1,)), ((), ())), preferred_element_type=F32)
    for h in range(heads):
        g, r = divmod(h, group)
        for i in range(nq):
            at = slice(i * QB, (i + 1) * QB)
            to = slice(r * QB, (r + 1) * QB)
            dlt[g, i, :, to] = jnp.broadcast_to(stat[h:h + 1, at], (8, QB))
            lse[g, i, :, to] = jnp.broadcast_to(stat[heads + h:heads + h + 1, at] * LOG2E, (8, QB))
    loads[2].wait()

    def q_block(i, _):
        hi = qpos_ref[i, 0:1, :]
        lo = qpos_ref[i, 1:2, :]

        def k_tile(t, _):
            rows = pl.ds(pl.multiple_of(t * KS, KS), KS)
            kp = kpos[:, rows, :].reshape(tile, HDIM)
            keep = jnp.where((kp <= hi) & (kp >= lo), 1.0, 0.0)
            keep = jnp.concatenate([keep] * group, axis=1) > 0.5
            for g in range(kvh):
                kc = slice(g * HDIM, (g + 1) * HDIM)
                vc = slice(kvw + g * HDIM, kvw + (g + 1) * HDIM)
                kt = all_ref[:, rows, kc].reshape(tile, HDIM)
                vt = all_ref[:, rows, vc].reshape(tile, HDIM)
                qt = qs[g, i]
                gt = gs[g, i]
                last = (((1,), (1,)), ((), ()))
                s = lax.dot_general(kt, qt, last, preferred_element_type=F32)
                p = jnp.where(keep, jnp.exp2(s * (scale * LOG2E) - lse[g, i, 0:1, :]), 0.0)
                dp = lax.dot_general(vt, gt, last, preferred_element_type=F32)
                ds = (p * (dp - dlt[g, i, 0:1, :]) * scale).astype(BF)
                dkv[:, rows, vc] += dot(p.astype(BF), gt).reshape(NZ, KS, HDIM)
                dkv[:, rows, kc] += dot(ds, qt).reshape(NZ, KS, HDIM)
                dq[g, i] += dot_rows(ds, kt)
            return 0

        lax.fori_loop(span_ref[0, i], span_ref[1, i], k_tile, 0)
        return 0

    lax.fori_loop(0, nq, q_block, 0)
    dkv_ref[...] = dkv[...].astype(BF)
    for h in range(0, heads, 2):
        cols = []
        for e in range(2):
            g, r = divmod(h + e, group)
            cols.append(jnp.concatenate([dq[g, i, r * QB:(r + 1) * QB, :] for i in range(nq)], axis=0).astype(BF))
        dq_ref[:, h * HDIM:(h + 2) * HDIM] = dot_rows(pick, jnp.concatenate(cols, axis=1)).astype(BF)


def attend(span, tab, kv_all, rq, rg, idx_row, qpos, group, kvh):
    cap, kvw = kv_all.shape[1:]
    nq = qpos.shape[0]
    slots, width = rq.shape
    return pl.pallas_call(
        functools.partial(attend_kernel, group, kvh),
        out_shape=(
            jax.ShapeDtypeStruct((NZ, cap, kvw), BF),
            jax.ShapeDtypeStruct((slots, width), BF),
        ),
        in_specs=[SMEM_SPEC] * 2 + [ANY_SPEC] * 3 + [VMEM_SPEC] * 2,
        out_specs=(VMEM_SPEC, VMEM_SPEC),
        scratch_shapes=[
            pltpu.VMEM((NZ, cap, kvw), BF), pltpu.VMEM(rq.shape, BF), pltpu.VMEM(rg.shape, BF),
            pltpu.VMEM((kvh, nq, group * QB, HDIM), BF), pltpu.VMEM((kvh, nq, group * QB, HDIM), BF),
            pltpu.VMEM((kvh, nq, 8, group * QB), F32), pltpu.VMEM((kvh, nq, 8, group * QB), F32),
            pltpu.VMEM((kvh, nq, group * QB, HDIM), F32), pltpu.VMEM((NZ, cap, kvw), F32),
            pltpu.VMEM((NZ, cap, HDIM), jnp.int32),
            pltpu.SemaphoreType.DMA((3,)),
        ],
        compiler_params=pltpu.CompilerParams(vmem_limit_bytes=60 << 20),
        name="attention_grads",
    )(span, tab, kv_all, rq, rg, idx_row, qpos)


def return_kernel(dkv_hbm, dq_ref, idx_ref, rdq_ref, rdkv_ref, dkv_ref, fin, bin_, fout, bout, slots,
                  qs, qr, ks, kr, ls, fs, fr, bs, br):
    z = lax.axis_index("ctx")
    d = lax.axis_index("dp")
    cap, kvw = dkv_ref.shape[1:]
    part = cap // 2
    last = NZ // 2 - 1
    load = pltpu.make_async_copy(dkv_hbm, dkv_ref, ls.at[2])
    load.start()
    greet()
    sent = []

    def hop(step, piece):
        rows = pl.ds(piece * part, part)
        for by, owner, send, recv, into, out, half in (
                (1, lax.rem(z + NZ // 2 - step, NZ), fs, fr, fin, fout, 0),
                (NZ - 1, lax.rem(z + NZ // 2 + step, NZ), bs, br, bin_, bout, 1)):
            if step == 0 and piece != half:
                continue
            if step == 0 or (step == 1 and piece != half):
                src = dkv_hbm.at[owner, rows]
            else:
                for s, p, b, c in sent:
                    if s == step - 1 and p == piece and b == by:
                        c.wait_recv()
                out[step, rows, :] = (dkv_ref[owner, rows, :].astype(F32)
                                      + into[step - 1, rows, :].astype(F32)).astype(BF)
                src = out.at[step, rows]
            c = along(by, src, into.at[step, rows], send.at[step, piece], recv.at[step, piece])
            c.start()
            sent.append((step, piece, by, c))

    hop(0, 0)
    hop(0, 1)
    dq_copies = exchange(dq_ref, rdq_ref, qs, qr)
    for c in dq_copies:
        c.start()
    own = pltpu.make_async_copy(dq_ref.at[d], rdq_ref.at[d], ls.at[0])
    own.start()
    load.wait()
    for step in range(1, NZ // 2):
        hop(step, 0)
        hop(step, 1)
    for s, p, b, c in sent:
        if s == last:
            c.wait_recv()
    total = (dkv_ref[z].astype(F32) + fin[last].astype(F32) + bin_[last].astype(F32)).astype(BF)
    slots[...] = dot_rows(one_hot_rows(cap, idx_ref[...]), total).astype(BF).reshape(slots.shape)
    kv_copies = exchange(slots, rdkv_ref, ks, kr)
    for c in kv_copies:
        c.start()
    own_kv = pltpu.make_async_copy(slots.at[d], rdkv_ref.at[d], ls.at[1])
    own_kv.start()
    for s, p, b, c in sent:
        c.wait_send()
    own.wait()
    own_kv.wait()
    for c in dq_copies:
        c.wait()
    for c in kv_copies:
        c.wait()


def send_back(dkv, dq, idx_row, cid):
    cap, kvw = dkv.shape[1:]
    pair, width = dq.shape[1:]
    dma = pltpu.SemaphoreType.DMA
    return pl.pallas_call(
        return_kernel,
        out_shape=(
            jax.ShapeDtypeStruct((ND, pair, width), BF),
            jax.ShapeDtypeStruct((ND, pair, kvw), BF),
        ),
        in_specs=[ANY_SPEC, ANY_SPEC, VMEM_SPEC],
        out_specs=(ANY_SPEC, ANY_SPEC),
        scratch_shapes=[pltpu.VMEM((NZ, cap, kvw), BF)] + [pltpu.VMEM((NZ // 2, cap, kvw), BF)] * 4 + [
            pltpu.VMEM((ND, pair, kvw), BF),
            dma((ND,)), dma((ND,)), dma((ND,)), dma((ND,)), dma((3,)),
            dma((4, 2)), dma((4, 2)), dma((4, 2)), dma((4, 2)),
        ],
        compiler_params=pltpu.CompilerParams(
            collective_id=cid, has_side_effects=True, vmem_limit_bytes=56 << 20),
        name="return_rows",
    )(dkv, dq, idx_row)


def unpack_kernel(dq_ref, dkv_ref, slot_ref, gq_ref, gk_ref, gv_ref):
    slots, width = dq_ref.shape
    kvw = gk_ref.shape[1]
    pick = one_hot_rows(slots, slot_ref[...])
    for at in range(0, width, 2 * HDIM):
        gq_ref[:, at:at + 2 * HDIM] = dot_rows(pick, dq_ref[:, at:at + 2 * HDIM]).astype(BF)
    gk_ref[...] = dot_rows(pick, dkv_ref[:, :kvw]).astype(BF)
    gv_ref[...] = dot_rows(pick, dkv_ref[:, kvw:]).astype(BF)


def unpack(rdq, rdkv, slot_row):
    tok = slot_row.shape[1]
    slots = rdq.shape[0] * rdq.shape[1]
    width = rdq.shape[2]
    kvw = rdkv.shape[2] // 2
    return pl.pallas_call(
        unpack_kernel,
        out_shape=(
            jax.ShapeDtypeStruct((tok, width), BF),
            jax.ShapeDtypeStruct((tok, kvw), BF),
            jax.ShapeDtypeStruct((tok, kvw), BF),
        ),
        in_specs=[VMEM_SPEC] * 3,
        out_specs=(VMEM_SPEC,) * 3,
        compiler_params=pltpu.CompilerParams(vmem_limit_bytes=32 << 20),
        name="unpack_rows",
    )(rdq.reshape(slots, width), rdkv.reshape(slots, 2 * kvw), slot_row)


def body(query, keys, values, output, grad_out, log_norm, route_counts, doc_lengths):
    tok = query.shape[0]
    kvh = keys.shape[1] // HDIM
    group = query.shape[1] // keys.shape[1]
    loads = jnp.sum(route_counts.reshape(NZ, ND, NZ, ND), axis=2)
    fits = (jnp.max(jnp.sum(loads, axis=1)) <= FAST[0]) & (jnp.max(loads) <= FAST[1])

    def run(size, cid, *rows):
        cap, pair = size
        capq = -(-cap // QB) * QB
        q = plane_counts(route_counts)
        slot = source_slots(route_counts, tok, pair).reshape(1, -1)
        idx = compact_index(q, pair).reshape(1, -1)
        pos, tab = positions(q, cap, tok)
        mine = lax.dynamic_index_in_dim(pos, lax.axis_index("ctx"), 0, keepdims=False)
        mine = jnp.pad(mine, (0, capq - cap), constant_values=FAR)
        bounds = ends_of(doc_lengths[0], 0)
        lo = jnp.max(jnp.where(bounds[None, :] <= mine[:, None], bounds[None, :], 0), axis=1)
        hi = jnp.where(mine < FAR, mine, -1)
        qpos = jnp.stack([hi.reshape(-1, QB), lo.reshape(-1, QB)], axis=1)
        k_tiles = pos.reshape(NZ, -1, KS)
        k_min = jnp.min(k_tiles, axis=(0, 2))
        k_max = jnp.max(k_tiles, axis=(0, 2))
        q_max = jnp.max(qpos[:, 0, :], axis=1)
        q_min = jnp.min(jnp.where(qpos[:, 0, :] >= 0, qpos[:, 1, :], FAR), axis=1)
        span = jnp.stack([
            jnp.sum((k_max[None, :] < q_min[:, None]).astype(jnp.int32), axis=1),
            jnp.sum((k_min[None, :] <= q_max[:, None]).astype(jnp.int32), axis=1)])
        kv_all, rq, rg = dispatch(*rows, slot, idx, cap, pair, cid)
        slots = ND * pair
        dkv, dq = attend(span, tab, kv_all, rq.reshape(slots, -1), rg.reshape(slots, -1), idx, qpos, group, kvh)
        rdq, rdkv = send_back(dkv, dq.reshape(ND, pair, -1), idx, cid + 1)
        return unpack(rdq, rdkv, slot)

    return lax.cond(fits, functools.partial(run, FAST, 0), functools.partial(run, SLOW, 2),
                    query, keys, values, output, grad_out, log_norm)


def solution(mesh):
    rows = P(("ctx", "dp"), "head")
    return jax.shard_map(
        body, mesh=mesh, in_specs=(rows,) * 6 + (P(), P("dp", None)), out_specs=(rows,) * 3, check_vma=False)
```

```python
import functools

import jax
import jax.numpy as jnp
from jax import lax
from jax.experimental import pallas as pl
from jax.experimental.pallas import tpu as pltpu
from jax.sharding import PartitionSpec as P

HDIM = 128
NZ = 8
ND = 8
QB = 128
KS = 32
FAST = (448, 80)
SLOW = (704, 88)
FAR = 1 << 20
LOG2E = 1.4426950408889634
MESH = pl.DeviceIdType.MESH
BF = jnp.bfloat16
F32 = jnp.float32
VMEM_SPEC = pl.BlockSpec(memory_space=pltpu.VMEM)
SMEM_SPEC = pl.BlockSpec(memory_space=pltpu.SMEM)
ANY_SPEC = pl.BlockSpec(memory_space=pl.ANY)


def dot(a, b):
    return jnp.dot(a, b, preferred_element_type=F32)


def one_hot_rows(count, row):
    ids = lax.broadcasted_iota(jnp.int32, (count, row.shape[1]), 0)
    return jnp.where(ids == row, 1.0, 0.0).astype(BF)


def dot_rows(a, b):
    return lax.dot_general(a, b, (((0,), (0,)), ((), ())), preferred_element_type=F32)


def tables_kernel(tok, rc_ref, counts_ref, doc_ref, slot_ref, idx_ref, qpos_ref, tab_ref, span_ref, fits_ref, tops):
    z = lax.axis_index("ctx")
    d = lax.axis_index("dp")
    owners = NZ * ND
    part_of = lax.broadcasted_iota(jnp.int32, (owners, HDIM), 0) % ND
    lanes = lax.broadcasted_iota(jnp.int32, (owners, HDIM), 1)
    pairs = dot(counts_ref[...].astype(F32).astype(BF), jnp.where(part_of == lanes, 1.0, 0.0).astype(BF))
    plane = lax.broadcasted_iota(jnp.int32, (NZ, owners), 1) // ND
    loads = dot(jnp.where(plane == lax.broadcasted_iota(jnp.int32, (NZ, owners), 0), 1.0, 0.0).astype(BF),
                pairs.astype(BF))
    fits = (jnp.max(loads) <= FAST[0]) & (jnp.max(pairs) <= FAST[1])
    fits_ref[0] = fits.astype(jnp.int32)
    pair = jnp.where(fits, FAST[1], SLOW[1])

    ids = lax.broadcasted_iota(jnp.int32, (1, tok), 1)
    slot = ids
    start = jnp.int32(0)
    filled = [jnp.int32(0)] * ND
    for f in range(owners):
        n = rc_ref[z * ND + d, f]
        to = f % ND
        slot = jnp.where(ids >= start, ids + (to * pair + filled[to] - start), slot)
        filled[to] = filled[to] + n
        start = start + n
    slot_ref[...] = slot

    start = jnp.int32(0)
    for c in range(NZ):
        for e in range(ND):
            tops[e, c] = start
            start = start + rc_ref[z * ND + e, c * ND + d]
    ids = lax.broadcasted_iota(jnp.int32, idx_ref.shape, 1)
    idx = ids
    for e in range(ND):
        start = e * pair
        for c in range(NZ):
            idx = jnp.where(ids >= start, ids + (tops[e, c] - start), idx)
            start = start + rc_ref[z * ND + e, c * ND + d]
        idx = jnp.where(ids >= start, -1, idx)
    idx_ref[...] = idx

    before = [jnp.int32(0)] * NZ
    for c0 in range(NZ):
        start = jnp.int32(0)
        for c in range(NZ):
            n = rc_ref[c0 * ND, c * ND + d]
            for e in range(1, ND):
                n = n + rc_ref[c0 * ND + e, c * ND + d]
            tab_ref[c0, NZ + c] = c * tok + before[c] - start
            start = start + n
            before[c] = before[c] + n
            tab_ref[c0, c] = start

    def placed(ids, plane):
        pos = ids + tab_ref[plane, NZ]
        for c in range(1, NZ):
            pos = jnp.where(ids >= tab_ref[plane, c - 1], ids + tab_ref[plane, NZ + c], pos)
        return jnp.where(ids >= tab_ref[plane, NZ - 1], FAR, pos)

    first = lax.broadcasted_iota(jnp.int32, (1, HDIM), 1) * KS
    k_min = k_max = None
    for c0 in range(NZ):
        low, high = placed(first, c0), placed(first + (KS - 1), c0)
        k_min = low if c0 == 0 else jnp.minimum(k_min, low)
        k_max = high if c0 == 0 else jnp.maximum(k_max, high)
    for b in range(qpos_ref.shape[0]):
        pos = placed(lax.broadcasted_iota(jnp.int32, (1, QB), 1) + b * QB, z)
        lo = jnp.zeros_like(pos)
        bound = jnp.int32(0)
        for m in range(doc_ref.shape[1]):
            bound = bound + doc_ref[0, m]
            lo = jnp.where(pos >= bound, bound, lo)
        hi = jnp.where(pos < FAR, pos, -1)
        qpos_ref[b, 0:1, :] = hi
        qpos_ref[b, 1:2, :] = lo
        q_max = jnp.max(hi.astype(F32)).astype(jnp.int32)
        q_min = jnp.min(jnp.where(pos < FAR, lo, FAR).astype(F32)).astype(jnp.int32)
        span_ref[0, b] = jnp.sum(jnp.where(k_max < q_min, 1.0, 0.0)).astype(jnp.int32)
        span_ref[1, b] = jnp.sum(jnp.where(k_min <= q_max, 1.0, 0.0)).astype(jnp.int32)


def tables(route_counts, doc_lengths, tok):
    blocks = -(-SLOW[0] // QB)
    i32 = jnp.int32
    return pl.pallas_call(
        functools.partial(tables_kernel, tok),
        out_shape=(
            jax.ShapeDtypeStruct((1, tok), i32), jax.ShapeDtypeStruct((1, ND * SLOW[1]), i32),
            jax.ShapeDtypeStruct((blocks, 2, QB), i32), jax.ShapeDtypeStruct((NZ, 2 * NZ), i32),
            jax.ShapeDtypeStruct((2, blocks), i32), jax.ShapeDtypeStruct((1,), i32),
        ),
        in_specs=[SMEM_SPEC, VMEM_SPEC, SMEM_SPEC],
        out_specs=(VMEM_SPEC,) * 3 + (SMEM_SPEC,) * 3,
        scratch_shapes=[pltpu.SMEM((ND, NZ), i32)],
        name="routing_tables",
    )(route_counts, route_counts, doc_lengths)


def greet():
    z = lax.axis_index("ctx")
    d = lax.axis_index("dp")
    barrier = pltpu.get_barrier_semaphore()
    for s in range(1, ND):
        pl.semaphore_signal(barrier, inc=1, device_id={"dp": lax.rem(d + s, ND)}, device_id_type=MESH)
    for s in (1, NZ - 1):
        pl.semaphore_signal(barrier, inc=1, device_id={"ctx": lax.rem(z + s, NZ)}, device_id_type=MESH)
    pl.semaphore_wait(barrier, ND + 1)


def exchange(src, dst, send, recv):
    d = lax.axis_index("dp")
    copies = []
    for s in range(1, ND):
        to = lax.rem(d + s, ND)
        copies.append(pltpu.make_async_remote_copy(
            src_ref=src.at[to], dst_ref=dst.at[d], send_sem=send.at[s], recv_sem=recv.at[s],
            device_id={"dp": to}, device_id_type=MESH))
    return copies


def along(axis_by, src, dst, send, recv):
    z = lax.axis_index("ctx")
    return pltpu.make_async_remote_copy(
        src_ref=src, dst_ref=dst, send_sem=send, recv_sem=recv,
        device_id={"ctx": lax.rem(z + axis_by, NZ)}, device_id_type=MESH)


def dispatch_kernel(q_ref, k_ref, v_ref, o_ref, g_ref, l_ref, slot_ref, idx_ref, all_ref, rq_ref, rg_ref,
                    qv, kvv, ov, gv, stat, skv, sq, sg, rkv, mine,
                    ins, ks, kr, qs, qr, gs, gr, ls, fs, fr, bs, br):
    z = lax.axis_index("ctx")
    d = lax.axis_index("dp")
    width = qv.shape[1]
    heads = width // HDIM
    kvw = k_ref.shape[1]
    slots, pair = skv.shape[0] * skv.shape[1], skv.shape[1]
    cap = mine.shape[0]
    part = cap // 2
    loads = []
    for n, (src, dst) in enumerate(((k_ref, kvv.at[:, :kvw]), (v_ref, kvv.at[:, kvw:]),
                                    (q_ref, qv), (g_ref, gv), (o_ref, ov))):
        c = pltpu.make_async_copy(src, dst, ins.at[n])
        c.start()
        loads.append(c)
    greet()
    pick = one_hot_rows(slots, slot_ref[...])
    loads[0].wait()
    loads[1].wait()
    skv[...] = dot(pick, kvv[...]).astype(BF).reshape(skv.shape)
    kv_copies = exchange(skv, rkv, ks, kr)
    for c in kv_copies:
        c.start()
    own = [pltpu.make_async_copy(skv.at[d], rkv.at[d], ls.at[0])]
    own[0].start()
    loads[2].wait()
    for at in range(0, width, 2 * HDIM):
        at = slice(at, at + 2 * HDIM)
        sq[:, :, at] = dot(pick, qv[:, at]).astype(BF).reshape(ND, pair, 2 * HDIM)
    q_copies = exchange(sq, rq_ref, qs, qr)
    for c in q_copies:
        c.start()
    own.append(pltpu.make_async_copy(sq.at[d], rq_ref.at[d], ls.at[1]))
    own[1].start()
    loads[3].wait()
    loads[4].wait()
    stat[...] = jnp.zeros_like(stat)
    for h in range(heads):
        at = slice(h * HDIM, (h + 1) * HDIM)
        both = gv[:, at].astype(F32) * ov[:, at].astype(F32)
        stat[:, h:h + 1] = jnp.sum(both, axis=1, keepdims=True)
    for at in range(0, width, 2 * HDIM):
        at = slice(at, at + 2 * HDIM)
        sg[:, :, at] = dot(pick, gv[:, at]).astype(BF).reshape(ND, pair, 2 * HDIM)
    sg[:, :, width:] = dot(pick, stat[...].astype(BF)).astype(BF).reshape(ND, pair, HDIM)
    lse = lax.dot_general(pick, l_ref[...], (((1,), (1,)), ((), ())), preferred_element_type=F32)
    sg[:, :, width + heads:width + 2 * heads] = lse.astype(BF).reshape(ND, pair, heads)
    g_copies = exchange(sg, rg_ref, gs, gr)
    for c in g_copies:
        c.start()
    own.append(pltpu.make_async_copy(sg.at[d], rg_ref.at[d], ls.at[2]))
    own[2].start()
    own[0].wait()
    for c in kv_copies:
        c.wait_recv()
    mine[...] = dot(one_hot_rows(cap, idx_ref[:, :slots]), rkv[...].reshape(slots, 2 * kvw)).astype(BF)
    sent = []

    def hop(step, piece):
        rows = pl.ds(piece * part, part)
        for by, origin, send, recv, half in (
                (1, lax.rem(z - step + NZ, NZ), fs, fr, 0), (NZ - 1, lax.rem(z + step, NZ), bs, br, 1)):
            if step == NZ // 2 - 1 and piece != half:
                continue
            src = mine.at[rows] if step == 0 else all_ref.at[origin, rows]
            c = along(by, src, all_ref.at[origin, rows], send.at[step, piece], recv.at[step, piece])
            c.start()
            sent.append((step, piece, c))

    for piece in range(2):
        hop(0, piece)
    own.append(pltpu.make_async_copy(mine, all_ref.at[z], ls.at[3]))
    own[3].start()
    for step in range(1, NZ // 2):
        for piece in range(2):
            for s, p, c in list(sent):
                if s == step - 1 and p == piece:
                    c.wait_recv()
            hop(step, piece)
    for s, p, c in sent:
        if s == NZ // 2 - 1:
            c.wait_recv()
        c.wait_send()
    for c in kv_copies:
        c.wait_send()
    for c in q_copies + g_copies:
        c.wait()
    for c in own[1:]:
        c.wait()


def dispatch(query, keys, values, output, grad_out, log_norm, slot_row, idx_row, cap, pair, cid):
    tok, width = query.shape
    kvw = 2 * keys.shape[1]
    gw = width + HDIM
    dma = pltpu.SemaphoreType.DMA
    return pl.pallas_call(
        dispatch_kernel,
        out_shape=(
            jax.ShapeDtypeStruct((NZ, cap, kvw), BF),
            jax.ShapeDtypeStruct((ND, pair, width), BF),
            jax.ShapeDtypeStruct((ND, pair, gw), BF),
        ),
        in_specs=[ANY_SPEC] * 5 + [VMEM_SPEC] * 3,
        out_specs=(ANY_SPEC,) * 3,
        scratch_shapes=[
            pltpu.VMEM((tok, width), BF), pltpu.VMEM((tok, kvw), BF),
            pltpu.VMEM((tok, width), BF), pltpu.VMEM((tok, width), BF), pltpu.VMEM((tok, HDIM), F32),
            pltpu.VMEM((ND, pair, kvw), BF), pltpu.VMEM((ND, pair, width), BF), pltpu.VMEM((ND, pair, gw), BF),
            pltpu.VMEM((ND, pair, kvw), BF), pltpu.VMEM((cap, kvw), BF),
            dma((5,)), dma((ND,)), dma((ND,)), dma((ND,)), dma((ND,)), dma((ND,)), dma((ND,)), dma((4,)),
            dma((4, 2)), dma((4, 2)), dma((4, 2)), dma((4, 2)),
        ],
        compiler_params=pltpu.CompilerParams(
            collective_id=cid, has_side_effects=True, vmem_limit_bytes=56 << 20),
        name="dispatch_rows",
    )(query, keys, values, output, grad_out, log_norm.T, slot_row, idx_row)


def attend_kernel(group, kvh, span_ref, tab_ref, all_hbm, rq_hbm, rg_hbm, row_ref, qpos_ref, dkv_ref, dq_ref,
                  all_ref, rq_ref, rg_ref, qs, gs, lse, dlt, dq, dkv, kpos, ins):
    nq = qs.shape[1]
    capq = nq * QB
    heads = group * kvh
    width = heads * HDIM
    kvw = kvh * HDIM
    scale = HDIM ** -0.5
    cap = all_ref.shape[1]
    tile = NZ * KS
    loads = []
    for n, (src, dst) in enumerate(((rq_hbm, rq_ref), (rg_hbm, rg_ref), (all_hbm, all_ref))):
        c = pltpu.make_async_copy(src, dst, ins.at[n])
        c.start()
        loads.append(c)
    pick = one_hot_rows(capq, row_ref[:, :rq_ref.shape[0]])
    ids = lax.broadcasted_iota(jnp.int32, (cap, HDIM), 0)
    for z in range(NZ):
        p = ids + tab_ref[z, NZ]
        for c in range(NZ):
            jump = tab_ref[z, NZ + c + 1] - tab_ref[z, NZ + c] if c + 1 < NZ else FAR
            p = p + jnp.where(ids >= tab_ref[z, c], jump, 0)
        kpos[z] = p
    dq[...] = jnp.zeros_like(dq)
    dkv[...] = jnp.zeros_like(dkv)
    for load, src, dst in ((loads[0], rq_ref, qs), (loads[1], rg_ref, gs)):
        load.wait()
        for h in range(0, heads, 2):
            both = dot(pick, src[:, h * HDIM:(h + 2) * HDIM]).astype(BF)
            for e in range(2):
                g, r = divmod(h + e, group)
                for i in range(nq):
                    dst[g, i, r * QB:(r + 1) * QB, :] = both[i * QB:(i + 1) * QB, e * HDIM:(e + 1) * HDIM]
    stat = lax.dot_general(rg_ref[:, width:], pick, (((0,), (1,)), ((), ())), preferred_element_type=F32)
    for h in range(heads):
        g, r = divmod(h, group)
        for i in range(nq):
            at = slice(i * QB, (i + 1) * QB)
            to = slice(r * QB, (r + 1) * QB)
            dlt[g, i, :, to] = jnp.broadcast_to(stat[h:h + 1, at], (8, QB))
            lse[g, i, :, to] = jnp.broadcast_to(stat[heads + h:heads + h + 1, at] * LOG2E, (8, QB))
    loads[2].wait()

    def q_block(i, _):
        hi = qpos_ref[i, 0:1, :]
        lo = qpos_ref[i, 1:2, :]

        def k_tile(t, _):
            rows = pl.ds(pl.multiple_of(t * KS, KS), KS)
            kp = kpos[:, rows, :].reshape(tile, HDIM)
            keep = jnp.where((kp <= hi) & (kp >= lo), 1.0, 0.0)
            keep = jnp.concatenate([keep] * group, axis=1) > 0.5
            for g in range(kvh):
                kc = slice(g * HDIM, (g + 1) * HDIM)
                vc = slice(kvw + g * HDIM, kvw + (g + 1) * HDIM)
                kt = all_ref[:, rows, kc].reshape(tile, HDIM)
                vt = all_ref[:, rows, vc].reshape(tile, HDIM)
                qt = qs[g, i]
                gt = gs[g, i]
                last = (((1,), (1,)), ((), ()))
                s = lax.dot_general(kt, qt, last, preferred_element_type=F32)
                p = jnp.where(keep, jnp.exp2(s * (scale * LOG2E) - lse[g, i, 0:1, :]), 0.0)
                dp = lax.dot_general(vt, gt, last, preferred_element_type=F32)
                ds = (p * (dp - dlt[g, i, 0:1, :]) * scale).astype(BF)
                dkv[:, rows, vc] += dot(p.astype(BF), gt).reshape(NZ, KS, HDIM)
                dkv[:, rows, kc] += dot(ds, qt).reshape(NZ, KS, HDIM)
                dq[g, i] += dot_rows(ds, kt)
            return 0

        lax.fori_loop(span_ref[0, i], span_ref[1, i], k_tile, 0)
        return 0

    lax.fori_loop(0, nq, q_block, 0)
    dkv_ref[...] = dkv[...].astype(BF)
    back = pick.T
    for h in range(0, heads, 2):
        cols = []
        for e in range(2):
            g, r = divmod(h + e, group)
            cols.append(jnp.concatenate([dq[g, i, r * QB:(r + 1) * QB, :] for i in range(nq)], axis=0).astype(BF))
        dq_ref[:, h * HDIM:(h + 2) * HDIM] = dot(back, jnp.concatenate(cols, axis=1)).astype(BF)


def attend(span, tab, kv_all, rq, rg, idx_row, qpos, group, kvh):
    cap, kvw = kv_all.shape[1:]
    nq = -(-cap // QB)
    slots, width = rq.shape
    return pl.pallas_call(
        functools.partial(attend_kernel, group, kvh),
        out_shape=(
            jax.ShapeDtypeStruct((NZ, cap, kvw), BF),
            jax.ShapeDtypeStruct((slots, width), BF),
        ),
        in_specs=[SMEM_SPEC] * 2 + [ANY_SPEC] * 3 + [VMEM_SPEC] * 2,
        out_specs=(VMEM_SPEC, VMEM_SPEC),
        scratch_shapes=[
            pltpu.VMEM((NZ, cap, kvw), BF), pltpu.VMEM(rq.shape, BF), pltpu.VMEM(rg.shape, BF),
            pltpu.VMEM((kvh, nq, group * QB, HDIM), BF), pltpu.VMEM((kvh, nq, group * QB, HDIM), BF),
            pltpu.VMEM((kvh, nq, 8, group * QB), F32), pltpu.VMEM((kvh, nq, 8, group * QB), F32),
            pltpu.VMEM((kvh, nq, group * QB, HDIM), F32), pltpu.VMEM((NZ, cap, kvw), F32),
            pltpu.VMEM((NZ, cap, HDIM), jnp.int32),
            pltpu.SemaphoreType.DMA((3,)),
        ],
        compiler_params=pltpu.CompilerParams(vmem_limit_bytes=60 << 20),
        name="attention_grads",
    )(span, tab, kv_all, rq, rg, idx_row, qpos)


def return_kernel(dkv_hbm, dq_ref, idx_ref, rdq_ref, rdkv_ref, dkv_ref, fin, bin_, fout, bout, slots,
                  qs, qr, ks, kr, ls, fs, fr, bs, br):
    z = lax.axis_index("ctx")
    d = lax.axis_index("dp")
    cap, kvw = dkv_ref.shape[1:]
    part = cap // 2
    last = NZ // 2 - 1
    load = pltpu.make_async_copy(dkv_hbm, dkv_ref, ls.at[2])
    load.start()
    greet()
    sent = []

    def hop(step, piece):
        rows = pl.ds(piece * part, part)
        for by, owner, send, recv, into, out, half in (
                (1, lax.rem(z + NZ // 2 - step, NZ), fs, fr, fin, fout, 0),
                (NZ - 1, lax.rem(z + NZ // 2 + step, NZ), bs, br, bin_, bout, 1)):
            if step == 0 and piece != half:
                continue
            if step == 0 or (step == 1 and piece != half):
                src = dkv_hbm.at[owner, rows]
            else:
                for s, p, b, c in sent:
                    if s == step - 1 and p == piece and b == by:
                        c.wait_recv()
                out[step, rows, :] = (dkv_ref[owner, rows, :].astype(F32)
                                      + into[step - 1, rows, :].astype(F32)).astype(BF)
                src = out.at[step, rows]
            c = along(by, src, into.at[step, rows], send.at[step, piece], recv.at[step, piece])
            c.start()
            sent.append((step, piece, by, c))

    hop(0, 0)
    hop(0, 1)
    dq_copies = exchange(dq_ref, rdq_ref, qs, qr)
    for c in dq_copies:
        c.start()
    own = pltpu.make_async_copy(dq_ref.at[d], rdq_ref.at[d], ls.at[0])
    own.start()
    load.wait()
    for step in range(1, NZ // 2):
        hop(step, 0)
        hop(step, 1)
    for s, p, b, c in sent:
        if s == last:
            c.wait_recv()
    total = (dkv_ref[z].astype(F32) + fin[last].astype(F32) + bin_[last].astype(F32)).astype(BF)
    slots[...] = dot_rows(one_hot_rows(cap, idx_ref[:, :ND * slots.shape[1]]), total).astype(BF).reshape(slots.shape)
    kv_copies = exchange(slots, rdkv_ref, ks, kr)
    for c in kv_copies:
        c.start()
    own_kv = pltpu.make_async_copy(slots.at[d], rdkv_ref.at[d], ls.at[1])
    own_kv.start()
    for s, p, b, c in sent:
        c.wait_send()
    own.wait()
    own_kv.wait()
    for c in dq_copies:
        c.wait()
    for c in kv_copies:
        c.wait()


def send_back(dkv, dq, idx_row, cid):
    cap, kvw = dkv.shape[1:]
    pair, width = dq.shape[1:]
    dma = pltpu.SemaphoreType.DMA
    return pl.pallas_call(
        return_kernel,
        out_shape=(
            jax.ShapeDtypeStruct((ND, pair, width), BF),
            jax.ShapeDtypeStruct((ND, pair, kvw), BF),
        ),
        in_specs=[ANY_SPEC, ANY_SPEC, VMEM_SPEC],
        out_specs=(ANY_SPEC, ANY_SPEC),
        scratch_shapes=[pltpu.VMEM((NZ, cap, kvw), BF)] + [pltpu.VMEM((NZ // 2, cap, kvw), BF)] * 4 + [
            pltpu.VMEM((ND, pair, kvw), BF),
            dma((ND,)), dma((ND,)), dma((ND,)), dma((ND,)), dma((3,)),
            dma((4, 2)), dma((4, 2)), dma((4, 2)), dma((4, 2)),
        ],
        compiler_params=pltpu.CompilerParams(
            collective_id=cid, has_side_effects=True, vmem_limit_bytes=56 << 20),
        name="return_rows",
    )(dkv, dq, idx_row)


def unpack_kernel(dq_hbm, dkv_hbm, slot_ref, gq_ref, gk_ref, gv_ref, dq_ref, dkv_ref, ins):
    slots, width = dq_ref.shape
    kvw = gk_ref.shape[1]
    blocks = range(0, width, 2 * HDIM)
    loads = [pltpu.make_async_copy(dkv_hbm, dkv_ref, ins.at[len(blocks)])]
    for n, at in enumerate(blocks):
        at = pl.ds(at, 2 * HDIM)
        loads.append(pltpu.make_async_copy(dq_hbm.at[:, at], dq_ref.at[:, at], ins.at[n]))
    for c in loads:
        c.start()
    pick = one_hot_rows(slots, slot_ref[...]).T
    loads[0].wait()
    gk_ref[...] = dot(pick, dkv_ref[:, :kvw]).astype(BF)
    gv_ref[...] = dot(pick, dkv_ref[:, kvw:]).astype(BF)
    for n, at in enumerate(blocks):
        loads[n + 1].wait()
        gq_ref[:, at:at + 2 * HDIM] = dot(pick, dq_ref[:, at:at + 2 * HDIM]).astype(BF)


def unpack(rdq, rdkv, slot_row):
    tok = slot_row.shape[1]
    slots = rdq.shape[0] * rdq.shape[1]
    width = rdq.shape[2]
    kvw = rdkv.shape[2] // 2
    return pl.pallas_call(
        unpack_kernel,
        out_shape=(
            jax.ShapeDtypeStruct((tok, width), BF),
            jax.ShapeDtypeStruct((tok, kvw), BF),
            jax.ShapeDtypeStruct((tok, kvw), BF),
        ),
        in_specs=[ANY_SPEC, ANY_SPEC, VMEM_SPEC],
        out_specs=(VMEM_SPEC,) * 3,
        scratch_shapes=[
            pltpu.VMEM((slots, width), BF), pltpu.VMEM((slots, 2 * kvw), BF),
            pltpu.SemaphoreType.DMA((width // (2 * HDIM) + 1,)),
        ],
        compiler_params=pltpu.CompilerParams(vmem_limit_bytes=56 << 20),
        name="unpack_rows",
    )(rdq.reshape(slots, width), rdkv.reshape(slots, 2 * kvw), slot_row)


def body(query, keys, values, output, grad_out, log_norm, route_counts, doc_lengths):
    tok = query.shape[0]
    kvh = keys.shape[1] // HDIM
    group = query.shape[1] // keys.shape[1]
    slot, idx, qpos, tab, span, fits = tables(route_counts, doc_lengths, tok)

    def run(size, cid, *rows):
        cap, pair = size
        slots = ND * pair
        kv_all, rq, rg = dispatch(*rows, slot, idx, cap, pair, cid)
        dkv, dq = attend(span, tab, kv_all, rq.reshape(slots, -1), rg.reshape(slots, -1), idx, qpos, group, kvh)
        rdq, rdkv = send_back(dkv, dq.reshape(ND, pair, -1), idx, cid + 1)
        return unpack(rdq, rdkv, slot)

    return lax.cond(fits[0] > 0, functools.partial(run, FAST, 0), functools.partial(run, SLOW, 2),
                    query, keys, values, output, grad_out, log_norm)


def solution(mesh):
    rows = P(("ctx", "dp"), "head")
    return jax.shard_map(
        body, mesh=mesh, in_specs=(rows,) * 6 + (P(), P("dp", None)), out_specs=(rows,) * 3, check_vma=False)
```

```python
import functools

import jax
import jax.numpy as jnp
from jax import lax
from jax.experimental import pallas as pl
from jax.experimental.pallas import tpu as pltpu
from jax.sharding import PartitionSpec as P

HDIM = 128
NZ = 8
ND = 8
QB = 128
KS = 32
FAST = (448, 80)
SLOW = (704, 88)
FAR = 1 << 20
LOG2E = 1.4426950408889634
MESH = pl.DeviceIdType.MESH
BF = jnp.bfloat16
F32 = jnp.float32
VMEM_SPEC = pl.BlockSpec(memory_space=pltpu.VMEM)
SMEM_SPEC = pl.BlockSpec(memory_space=pltpu.SMEM)
ANY_SPEC = pl.BlockSpec(memory_space=pl.ANY)


def dot(a, b):
    return jnp.dot(a, b, preferred_element_type=F32)


def one_hot_rows(count, row):
    ids = lax.broadcasted_iota(jnp.int32, (count, row.shape[1]), 0)
    return jnp.where(ids == row, 1.0, 0.0).astype(BF)


def dot_rows(a, b):
    return lax.dot_general(a, b, (((0,), (0,)), ((), ())), preferred_element_type=F32)


def tables_kernel(tok, rc_ref, counts_ref, doc_ref, slot_ref, idx_ref, qpos_ref, tab_ref, span_ref, fits_ref, tops):
    z = lax.axis_index("ctx")
    d = lax.axis_index("dp")
    owners = NZ * ND
    part_of = lax.broadcasted_iota(jnp.int32, (owners, HDIM), 0) % ND
    lanes = lax.broadcasted_iota(jnp.int32, (owners, HDIM), 1)
    pairs = dot(counts_ref[...].astype(F32).astype(BF), jnp.where(part_of == lanes, 1.0, 0.0).astype(BF))
    plane = lax.broadcasted_iota(jnp.int32, (NZ, owners), 1) // ND
    loads = dot(jnp.where(plane == lax.broadcasted_iota(jnp.int32, (NZ, owners), 0), 1.0, 0.0).astype(BF),
                pairs.astype(BF))
    fits = (jnp.max(loads) <= FAST[0]) & (jnp.max(pairs) <= FAST[1])
    fits_ref[0] = fits.astype(jnp.int32)
    pair = jnp.where(fits, FAST[1], SLOW[1])

    ids = lax.broadcasted_iota(jnp.int32, (1, tok), 1)
    slot = ids
    start = jnp.int32(0)
    filled = [jnp.int32(0)] * ND
    for f in range(owners):
        n = rc_ref[z * ND + d, f]
        to = f % ND
        slot = jnp.where(ids >= start, ids + (to * pair + filled[to] - start), slot)
        filled[to] = filled[to] + n
        start = start + n
    slot_ref[...] = slot

    start = jnp.int32(0)
    for c in range(NZ):
        for e in range(ND):
            tops[e, c] = start
            start = start + rc_ref[z * ND + e, c * ND + d]
    ids = lax.broadcasted_iota(jnp.int32, idx_ref.shape, 1)
    idx = ids
    for e in range(ND):
        start = e * pair
        for c in range(NZ):
            idx = jnp.where(ids >= start, ids + (tops[e, c] - start), idx)
            start = start + rc_ref[z * ND + e, c * ND + d]
        idx = jnp.where(ids >= start, -1, idx)
    idx_ref[...] = idx

    before = [jnp.int32(0)] * NZ
    for c0 in range(NZ):
        start = jnp.int32(0)
        for c in range(NZ):
            n = rc_ref[c0 * ND, c * ND + d]
            for e in range(1, ND):
                n = n + rc_ref[c0 * ND + e, c * ND + d]
            tab_ref[c0, NZ + c] = c * tok + before[c] - start
            start = start + n
            before[c] = before[c] + n
            tab_ref[c0, c] = start

    def placed(ids, plane):
        pos = ids + tab_ref[plane, NZ]
        for c in range(1, NZ):
            pos = jnp.where(ids >= tab_ref[plane, c - 1], ids + tab_ref[plane, NZ + c], pos)
        return jnp.where(ids >= tab_ref[plane, NZ - 1], FAR, pos)

    first = lax.broadcasted_iota(jnp.int32, (1, HDIM), 1) * KS
    k_min = k_max = None
    for c0 in range(NZ):
        low, high = placed(first, c0), placed(first + (KS - 1), c0)
        k_min = low if c0 == 0 else jnp.minimum(k_min, low)
        k_max = high if c0 == 0 else jnp.maximum(k_max, high)
    for b in range(qpos_ref.shape[0]):
        pos = placed(lax.broadcasted_iota(jnp.int32, (1, QB), 1) + b * QB, z)
        lo = jnp.zeros_like(pos)
        bound = jnp.int32(0)
        for m in range(doc_ref.shape[1]):
            bound = bound + doc_ref[0, m]
            lo = jnp.where(pos >= bound, bound, lo)
        hi = jnp.where(pos < FAR, pos, -1)
        qpos_ref[b, 0:1, :] = hi
        qpos_ref[b, 1:2, :] = lo
        q_max = jnp.max(hi.astype(F32)).astype(jnp.int32)
        q_min = jnp.min(jnp.where(pos < FAR, lo, FAR).astype(F32)).astype(jnp.int32)
        span_ref[0, b] = jnp.sum(jnp.where(k_max < q_min, 1.0, 0.0)).astype(jnp.int32)
        span_ref[1, b] = jnp.sum(jnp.where(k_min <= q_max, 1.0, 0.0)).astype(jnp.int32)


def tables(route_counts, doc_lengths, tok):
    blocks = -(-SLOW[0] // QB)
    i32 = jnp.int32
    return pl.pallas_call(
        functools.partial(tables_kernel, tok),
        out_shape=(
            jax.ShapeDtypeStruct((1, tok), i32), jax.ShapeDtypeStruct((1, ND * SLOW[1]), i32),
            jax.ShapeDtypeStruct((blocks, 2, QB), i32), jax.ShapeDtypeStruct((NZ, 2 * NZ), i32),
            jax.ShapeDtypeStruct((2, blocks), i32), jax.ShapeDtypeStruct((1,), i32),
        ),
        in_specs=[SMEM_SPEC, VMEM_SPEC, SMEM_SPEC],
        out_specs=(VMEM_SPEC,) * 3 + (SMEM_SPEC,) * 3,
        scratch_shapes=[pltpu.SMEM((ND, NZ), i32)],
        name="routing_tables",
    )(route_counts, route_counts, doc_lengths)


def greet():
    z = lax.axis_index("ctx")
    d = lax.axis_index("dp")
    barrier = pltpu.get_barrier_semaphore()
    for s in range(1, ND):
        pl.semaphore_signal(barrier, inc=1, device_id={"dp": lax.rem(d + s, ND)}, device_id_type=MESH)
    for s in (1, NZ - 1):
        pl.semaphore_signal(barrier, inc=1, device_id={"ctx": lax.rem(z + s, NZ)}, device_id_type=MESH)
    pl.semaphore_wait(barrier, ND + 1)


def exchange(src, dst, send, recv):
    d = lax.axis_index("dp")
    copies = []
    for s in range(1, ND):
        to = lax.rem(d + s, ND)
        copies.append(pltpu.make_async_remote_copy(
            src_ref=src.at[to], dst_ref=dst.at[d], send_sem=send.at[s], recv_sem=recv.at[s],
            device_id={"dp": to}, device_id_type=MESH))
    return copies


def along(axis_by, src, dst, send, recv):
    z = lax.axis_index("ctx")
    return pltpu.make_async_remote_copy(
        src_ref=src, dst_ref=dst, send_sem=send, recv_sem=recv,
        device_id={"ctx": lax.rem(z + axis_by, NZ)}, device_id_type=MESH)


def dispatch_kernel(q_ref, k_ref, v_ref, o_ref, g_ref, l_ref, slot_ref, idx_ref, all_ref, rq_ref, rg_ref,
                    qv, kvv, ov, gv, stat, skv, sq, sg, rkv, mine,
                    ins, ks, kr, qs, qr, gs, gr, ls, fs, fr, bs, br):
    z = lax.axis_index("ctx")
    d = lax.axis_index("dp")
    width = qv.shape[1]
    heads = width // HDIM
    kvw = k_ref.shape[1]
    slots, pair = skv.shape[0] * skv.shape[1], skv.shape[1]
    cap = mine.shape[0]
    part = cap // 2
    loads = []
    for n, (src, dst) in enumerate(((k_ref, kvv.at[:, :kvw]), (v_ref, kvv.at[:, kvw:]),
                                    (q_ref, qv), (g_ref, gv), (o_ref, ov))):
        c = pltpu.make_async_copy(src, dst, ins.at[n])
        c.start()
        loads.append(c)
    greet()
    pick = one_hot_rows(slots, slot_ref[...])
    loads[0].wait()
    loads[1].wait()
    skv[...] = dot(pick, kvv[...]).astype(BF).reshape(skv.shape)
    kv_copies = exchange(skv, rkv, ks, kr)
    for c in kv_copies:
        c.start()
    own = [pltpu.make_async_copy(skv.at[d], rkv.at[d], ls.at[0])]
    own[0].start()
    loads[2].wait()
    for at in range(0, width, 2 * HDIM):
        at = slice(at, at + 2 * HDIM)
        sq[:, :, at] = dot(pick, qv[:, at]).astype(BF).reshape(ND, pair, 2 * HDIM)
    q_copies = exchange(sq, rq_ref, qs, qr)
    for c in q_copies:
        c.start()
    own.append(pltpu.make_async_copy(sq.at[d], rq_ref.at[d], ls.at[1]))
    own[1].start()
    loads[3].wait()
    loads[4].wait()
    stat[...] = jnp.zeros_like(stat)
    for h in range(heads):
        at = slice(h * HDIM, (h + 1) * HDIM)
        both = gv[:, at].astype(F32) * ov[:, at].astype(F32)
        stat[:, h:h + 1] = jnp.sum(both, axis=1, keepdims=True)
    for at in range(0, width, 2 * HDIM):
        at = slice(at, at + 2 * HDIM)
        sg[:, :, at] = dot(pick, gv[:, at]).astype(BF).reshape(ND, pair, 2 * HDIM)
    sg[:, :, width:] = dot(pick, stat[...].astype(BF)).astype(BF).reshape(ND, pair, HDIM)
    lse = lax.dot_general(pick, l_ref[...], (((1,), (1,)), ((), ())), preferred_element_type=F32)
    sg[:, :, width + heads:width + 2 * heads] = lse.astype(BF).reshape(ND, pair, heads)
    g_copies = exchange(sg, rg_ref, gs, gr)
    for c in g_copies:
        c.start()
    own.append(pltpu.make_async_copy(sg.at[d], rg_ref.at[d], ls.at[2]))
    own[2].start()
    own[0].wait()
    for c in kv_copies:
        c.wait_recv()
    mine[...] = dot(one_hot_rows(cap, idx_ref[:, :slots]), rkv[...].reshape(slots, 2 * kvw)).astype(BF)
    sent = []

    def hop(step, piece):
        rows = pl.ds(piece * part, part)
        for by, origin, send, recv, half in (
                (1, lax.rem(z - step + NZ, NZ), fs, fr, 0), (NZ - 1, lax.rem(z + step, NZ), bs, br, 1)):
            if step == NZ // 2 - 1 and piece != half:
                continue
            src = mine.at[rows] if step == 0 else all_ref.at[origin, rows]
            c = along(by, src, all_ref.at[origin, rows], send.at[step, piece], recv.at[step, piece])
            c.start()
            sent.append((step, piece, c))

    for piece in range(2):
        hop(0, piece)
    own.append(pltpu.make_async_copy(mine, all_ref.at[z], ls.at[3]))
    own[3].start()
    for step in range(1, NZ // 2):
        for piece in range(2):
            for s, p, c in list(sent):
                if s == step - 1 and p == piece:
                    c.wait_recv()
            hop(step, piece)
    for s, p, c in sent:
        if s == NZ // 2 - 1:
            c.wait_recv()
        c.wait_send()
    for c in kv_copies:
        c.wait_send()
    for c in q_copies + g_copies:
        c.wait()
    for c in own[1:]:
        c.wait()


def dispatch(query, keys, values, output, grad_out, log_norm, slot_row, idx_row, cap, pair, cid):
    tok, width = query.shape
    kvw = 2 * keys.shape[1]
    gw = width + HDIM
    dma = pltpu.SemaphoreType.DMA
    return pl.pallas_call(
        dispatch_kernel,
        out_shape=(
            jax.ShapeDtypeStruct((NZ, cap, kvw), BF),
            jax.ShapeDtypeStruct((ND, pair, width), BF),
            jax.ShapeDtypeStruct((ND, pair, gw), BF),
        ),
        in_specs=[ANY_SPEC] * 5 + [VMEM_SPEC] * 3,
        out_specs=(ANY_SPEC,) * 3,
        scratch_shapes=[
            pltpu.VMEM((tok, width), BF), pltpu.VMEM((tok, kvw), BF),
            pltpu.VMEM((tok, width), BF), pltpu.VMEM((tok, width), BF), pltpu.VMEM((tok, HDIM), F32),
            pltpu.VMEM((ND, pair, kvw), BF), pltpu.VMEM((ND, pair, width), BF), pltpu.VMEM((ND, pair, gw), BF),
            pltpu.VMEM((ND, pair, kvw), BF), pltpu.VMEM((cap, kvw), BF),
            dma((5,)), dma((ND,)), dma((ND,)), dma((ND,)), dma((ND,)), dma((ND,)), dma((ND,)), dma((4,)),
            dma((4, 2)), dma((4, 2)), dma((4, 2)), dma((4, 2)),
        ],
        compiler_params=pltpu.CompilerParams(
            collective_id=cid, has_side_effects=True, vmem_limit_bytes=56 << 20),
        name="dispatch_rows",
    )(query, keys, values, output, grad_out, log_norm.T, slot_row, idx_row)


def attend_kernel(group, kvh, span_ref, tab_ref, all_hbm, rq_hbm, rg_hbm, row_ref, qpos_ref, dkv_hbm, dq_hbm,
                  all_ref, rq_ref, rg_ref, qs, gs, lse, dlt, dq, dkv, kpos, dkv_ref, dq_ref, ins):
    nq = qs.shape[1]
    capq = nq * QB
    heads = group * kvh
    width = heads * HDIM
    kvw = kvh * HDIM
    scale = HDIM ** -0.5
    cap = all_ref.shape[1]
    tile = NZ * KS
    loads = []
    for n, (src, dst) in enumerate(((rq_hbm, rq_ref), (rg_hbm, rg_ref), (all_hbm, all_ref))):
        c = pltpu.make_async_copy(src, dst, ins.at[n])
        c.start()
        loads.append(c)
    pick = one_hot_rows(capq, row_ref[:, :rq_ref.shape[0]])
    ids = lax.broadcasted_iota(jnp.int32, (cap, HDIM), 0)
    for z in range(NZ):
        p = ids + tab_ref[z, NZ]
        for c in range(NZ):
            jump = tab_ref[z, NZ + c + 1] - tab_ref[z, NZ + c] if c + 1 < NZ else FAR
            p = p + jnp.where(ids >= tab_ref[z, c], jump, 0)
        kpos[z] = p
    dq[...] = jnp.zeros_like(dq)
    dkv[...] = jnp.zeros_like(dkv)
    for load, src, dst in ((loads[0], rq_ref, qs), (loads[1], rg_ref, gs)):
        load.wait()
        for h in range(0, heads, 2):
            both = dot(pick, src[:, h * HDIM:(h + 2) * HDIM]).astype(BF)
            for e in range(2):
                g, r = divmod(h + e, group)
                for i in range(nq):
                    dst[g, i, r * QB:(r + 1) * QB, :] = both[i * QB:(i + 1) * QB, e * HDIM:(e + 1) * HDIM]
    stat = lax.dot_general(rg_ref[:, width:], pick, (((0,), (1,)), ((), ())), preferred_element_type=F32)
    for h in range(heads):
        g, r = divmod(h, group)
        for i in range(nq):
            at = slice(i * QB, (i + 1) * QB)
            to = slice(r * QB, (r + 1) * QB)
            dlt[g, i, :, to] = jnp.broadcast_to(stat[h:h + 1, at], (8, QB))
            lse[g, i, :, to] = jnp.broadcast_to(stat[heads + h:heads + h + 1, at] * LOG2E, (8, QB))
    loads[2].wait()

    def q_block(i, _):
        hi = qpos_ref[i, 0:1, :]
        lo = qpos_ref[i, 1:2, :]

        def k_tile(t, _):
            rows = pl.ds(pl.multiple_of(t * KS, KS), KS)
            kp = kpos[:, rows, :].reshape(tile, HDIM)
            keep = jnp.where((kp <= hi) & (kp >= lo), 1.0, 0.0)
            keep = jnp.concatenate([keep] * group, axis=1) > 0.5
            for g in range(kvh):
                kc = slice(g * HDIM, (g + 1) * HDIM)
                vc = slice(kvw + g * HDIM, kvw + (g + 1) * HDIM)
                kt = all_ref[:, rows, kc].reshape(tile, HDIM)
                vt = all_ref[:, rows, vc].reshape(tile, HDIM)
                qt = qs[g, i]
                gt = gs[g, i]
                last = (((1,), (1,)), ((), ()))
                s = lax.dot_general(kt, qt, last, preferred_element_type=F32)
                p = jnp.where(keep, jnp.exp2(s * (scale * LOG2E) - lse[g, i, 0:1, :]), 0.0)
                dp = lax.dot_general(vt, gt, last, preferred_element_type=F32)
                ds = (p * (dp - dlt[g, i, 0:1, :]) * scale).astype(BF)
                dkv[:, rows, vc] += dot(p.astype(BF), gt).reshape(NZ, KS, HDIM)
                dkv[:, rows, kc] += dot(ds, qt).reshape(NZ, KS, HDIM)
                dq[g, i] += dot_rows(ds, kt)
            return 0

        lax.fori_loop(span_ref[0, i], span_ref[1, i], k_tile, 0)
        return 0

    lax.fori_loop(0, nq, q_block, 0)
    dkv_ref[...] = dkv[...].astype(BF)
    outs = [pltpu.make_async_copy(dkv_ref, dkv_hbm, ins.at[3])]
    outs[0].start()
    back = pick.T
    for h in range(0, heads, 2):
        cols = []
        for e in range(2):
            g, r = divmod(h + e, group)
            cols.append(jnp.concatenate([dq[g, i, r * QB:(r + 1) * QB, :] for i in range(nq)], axis=0).astype(BF))
        dq_ref[:, h * HDIM:(h + 2) * HDIM] = dot(back, jnp.concatenate(cols, axis=1)).astype(BF)
    outs.append(pltpu.make_async_copy(dq_ref, dq_hbm, ins.at[4]))
    outs[1].start()
    for c in outs:
        c.wait()


def attend(span, tab, kv_all, rq, rg, idx_row, qpos, group, kvh):
    cap, kvw = kv_all.shape[1:]
    nq = -(-cap // QB)
    slots, width = rq.shape
    return pl.pallas_call(
        functools.partial(attend_kernel, group, kvh),
        out_shape=(
            jax.ShapeDtypeStruct((NZ, cap, kvw), BF),
            jax.ShapeDtypeStruct((slots, width), BF),
        ),
        in_specs=[SMEM_SPEC] * 2 + [ANY_SPEC] * 3 + [VMEM_SPEC] * 2,
        out_specs=(ANY_SPEC, ANY_SPEC),
        scratch_shapes=[
            pltpu.VMEM((NZ, cap, kvw), BF), pltpu.VMEM(rq.shape, BF), pltpu.VMEM(rg.shape, BF),
            pltpu.VMEM((kvh, nq, group * QB, HDIM), BF), pltpu.VMEM((kvh, nq, group * QB, HDIM), BF),
            pltpu.VMEM((kvh, nq, 8, group * QB), F32), pltpu.VMEM((kvh, nq, 8, group * QB), F32),
            pltpu.VMEM((kvh, nq, group * QB, HDIM), F32), pltpu.VMEM((NZ, cap, kvw), F32),
            pltpu.VMEM((NZ, cap, HDIM), jnp.int32),
            pltpu.VMEM((NZ, cap, kvw), BF), pltpu.VMEM((slots, width), BF),
            pltpu.SemaphoreType.DMA((5,)),
        ],
        compiler_params=pltpu.CompilerParams(vmem_limit_bytes=60 << 20),
        name="attention_grads",
    )(span, tab, kv_all, rq, rg, idx_row, qpos)


def return_kernel(dkv_hbm, dq_ref, idx_ref, slot_ref, gq_ref, gk_ref, gv_ref,
                  dkv_ref, fin, bin_, fout, bout, slots, rdq_ref, rdkv_ref, gq, gk, gv, qs, qr, ks, kr, ls, fs, fr, bs, br):
    z = lax.axis_index("ctx")
    d = lax.axis_index("dp")
    cap, kvw = dkv_ref.shape[1:]
    part = cap // 2
    last = NZ // 2 - 1
    load = pltpu.make_async_copy(dkv_hbm, dkv_ref, ls.at[2])
    load.start()
    greet()
    sent = []

    def hop(step, piece):
        rows = pl.ds(piece * part, part)
        for by, owner, send, recv, into, out, half in (
                (1, lax.rem(z + NZ // 2 - step, NZ), fs, fr, fin, fout, 0),
                (NZ - 1, lax.rem(z + NZ // 2 + step, NZ), bs, br, bin_, bout, 1)):
            if step == 0 and piece != half:
                continue
            if step == 0 or (step == 1 and piece != half):
                src = dkv_hbm.at[owner, rows]
            else:
                for s, p, b, c in sent:
                    if s == step - 1 and p == piece and b == by:
                        c.wait_recv()
                out[step, rows, :] = (dkv_ref[owner, rows, :].astype(F32)
                                      + into[step - 1, rows, :].astype(F32)).astype(BF)
                src = out.at[step, rows]
            c = along(by, src, into.at[step, rows], send.at[step, piece], recv.at[step, piece])
            c.start()
            sent.append((step, piece, by, c))

    hop(0, 0)
    hop(0, 1)
    dq_copies = exchange(dq_ref, rdq_ref, qs, qr)
    for c in dq_copies:
        c.start()
    own = pltpu.make_async_copy(dq_ref.at[d], rdq_ref.at[d], ls.at[0])
    own.start()
    load.wait()
    for step in range(1, NZ // 2):
        hop(step, 0)
        hop(step, 1)
    own.wait()
    for c in dq_copies:
        c.wait()
    count, width = slots.shape[0] * slots.shape[1], gq.shape[1]
    pick = one_hot_rows(count, slot_ref[...]).T
    rows = rdq_ref[...].reshape(count, width)
    gq[...] = dot(pick, rows).astype(BF)
    outs = [pltpu.make_async_copy(gq, gq_ref, ls.at[3])]
    outs[0].start()
    for s, p, b, c in sent:
        if s == last:
            c.wait_recv()
    total = (dkv_ref[z].astype(F32) + fin[last].astype(F32) + bin_[last].astype(F32)).astype(BF)
    slots[...] = dot_rows(one_hot_rows(cap, idx_ref[:, :ND * slots.shape[1]]), total).astype(BF).reshape(slots.shape)
    kv_copies = exchange(slots, rdkv_ref, ks, kr)
    for c in kv_copies:
        c.start()
    own_kv = pltpu.make_async_copy(slots.at[d], rdkv_ref.at[d], ls.at[1])
    own_kv.start()
    for s, p, b, c in sent:
        c.wait_send()
    own_kv.wait()
    for c in kv_copies:
        c.wait()
    rows = rdkv_ref[...].reshape(count, kvw)
    gk[...] = dot(pick, rows[:, :kvw // 2]).astype(BF)
    gv[...] = dot(pick, rows[:, kvw // 2:]).astype(BF)
    outs.append(pltpu.make_async_copy(gk, gk_ref, ls.at[4]))
    outs.append(pltpu.make_async_copy(gv, gv_ref, ls.at[5]))
    for c in outs[1:]:
        c.start()
    for c in outs:
        c.wait()


def send_back(dkv, dq, idx_row, slot_row, cid):
    cap, kvw = dkv.shape[1:]
    pair, width = dq.shape[1:]
    tok = slot_row.shape[1]
    dma = pltpu.SemaphoreType.DMA
    return pl.pallas_call(
        return_kernel,
        out_shape=(
            jax.ShapeDtypeStruct((tok, width), BF),
            jax.ShapeDtypeStruct((tok, kvw // 2), BF),
            jax.ShapeDtypeStruct((tok, kvw // 2), BF),
        ),
        in_specs=[ANY_SPEC, ANY_SPEC, VMEM_SPEC, VMEM_SPEC],
        out_specs=(ANY_SPEC,) * 3,
        scratch_shapes=[pltpu.VMEM((NZ, cap, kvw), BF)] + [pltpu.VMEM((NZ // 2, cap, kvw), BF)] * 4 + [
            pltpu.VMEM((ND, pair, kvw), BF), pltpu.VMEM((ND, pair, width), BF), pltpu.VMEM((ND, pair, kvw), BF),
            pltpu.VMEM((tok, width), BF), pltpu.VMEM((tok, kvw // 2), BF), pltpu.VMEM((tok, kvw // 2), BF),
            dma((ND,)), dma((ND,)), dma((ND,)), dma((ND,)), dma((6,)),
            dma((4, 2)), dma((4, 2)), dma((4, 2)), dma((4, 2)),
        ],
        compiler_params=pltpu.CompilerParams(
            collective_id=cid, has_side_effects=True, vmem_limit_bytes=56 << 20),
        name="return_rows",
    )(dkv, dq, idx_row, slot_row)


def body(query, keys, values, output, grad_out, log_norm, route_counts, doc_lengths):
    tok = query.shape[0]
    kvh = keys.shape[1] // HDIM
    group = query.shape[1] // keys.shape[1]
    slot, idx, qpos, tab, span, fits = tables(route_counts, doc_lengths, tok)

    def run(size, cid, *rows):
        cap, pair = size
        slots = ND * pair
        kv_all, rq, rg = dispatch(*rows, slot, idx, cap, pair, cid)
        dkv, dq = attend(span, tab, kv_all, rq.reshape(slots, -1), rg.reshape(slots, -1), idx, qpos, group, kvh)
        return send_back(dkv, dq.reshape(ND, pair, -1), idx, slot, cid + 1)

    return lax.cond(fits[0] > 0, functools.partial(run, FAST, 0), functools.partial(run, SLOW, 2),
                    query, keys, values, output, grad_out, log_norm)


def solution(mesh):
    rows = P(("ctx", "dp"), "head")
    return jax.shard_map(
        body, mesh=mesh, in_specs=(rows,) * 6 + (P(), P("dp", None)), out_specs=(rows,) * 3, check_vma=False)
```

```python
import functools

import jax
import jax.numpy as jnp
from jax import lax
from jax.experimental import pallas as pl
from jax.experimental.pallas import tpu as pltpu
from jax.sharding import PartitionSpec as P

HDIM = 128
NZ = 8
ND = 8
QB = 128
KS = 32
FAST = (448, 80)
SLOW = (704, 88)
FAR = 1 << 20
LOG2E = 1.4426950408889634
MESH = pl.DeviceIdType.MESH
BF = jnp.bfloat16
F32 = jnp.float32
VMEM_SPEC = pl.BlockSpec(memory_space=pltpu.VMEM)
SMEM_SPEC = pl.BlockSpec(memory_space=pltpu.SMEM)
ANY_SPEC = pl.BlockSpec(memory_space=pl.ANY)


def dot(a, b):
    return jnp.dot(a, b, preferred_element_type=F32)


def one_hot_rows(count, row):
    ids = lax.broadcasted_iota(jnp.int32, (count, row.shape[1]), 0)
    return jnp.where(ids == row, 1.0, 0.0).astype(BF)


def dot_rows(a, b):
    return lax.dot_general(a, b, (((0,), (0,)), ((), ())), preferred_element_type=F32)


def tables_kernel(tok, rc_ref, counts_ref, doc_ref, slot_ref, idx_ref, qpos_ref, tab_ref, span_ref, fits_ref, tops):
    z = lax.axis_index("ctx")
    d = lax.axis_index("dp")
    owners = NZ * ND
    part_of = lax.broadcasted_iota(jnp.int32, (owners, HDIM), 0) % ND
    lanes = lax.broadcasted_iota(jnp.int32, (owners, HDIM), 1)
    pairs = dot(counts_ref[...].astype(F32).astype(BF), jnp.where(part_of == lanes, 1.0, 0.0).astype(BF))
    plane = lax.broadcasted_iota(jnp.int32, (NZ, owners), 1) // ND
    loads = dot(jnp.where(plane == lax.broadcasted_iota(jnp.int32, (NZ, owners), 0), 1.0, 0.0).astype(BF),
                pairs.astype(BF))
    fits = (jnp.max(loads) <= FAST[0]) & (jnp.max(pairs) <= FAST[1])
    fits_ref[0] = fits.astype(jnp.int32)
    pair = jnp.where(fits, FAST[1], SLOW[1])

    ids = lax.broadcasted_iota(jnp.int32, (1, tok), 1)
    slot = ids
    start = jnp.int32(0)
    filled = [jnp.int32(0)] * ND
    for f in range(owners):
        n = rc_ref[z * ND + d, f]
        to = f % ND
        slot = jnp.where(ids >= start, ids + (to * pair + filled[to] - start), slot)
        filled[to] = filled[to] + n
        start = start + n
    slot_ref[...] = slot

    start = jnp.int32(0)
    for c in range(NZ):
        for e in range(ND):
            tops[e, c] = start
            start = start + rc_ref[z * ND + e, c * ND + d]
    ids = lax.broadcasted_iota(jnp.int32, idx_ref.shape, 1)
    idx = ids
    for e in range(ND):
        start = e * pair
        for c in range(NZ):
            idx = jnp.where(ids >= start, ids + (tops[e, c] - start), idx)
            start = start + rc_ref[z * ND + e, c * ND + d]
        idx = jnp.where(ids >= start, -1, idx)
    idx_ref[...] = idx

    before = [jnp.int32(0)] * NZ
    for c0 in range(NZ):
        start = jnp.int32(0)
        for c in range(NZ):
            n = rc_ref[c0 * ND, c * ND + d]
            for e in range(1, ND):
                n = n + rc_ref[c0 * ND + e, c * ND + d]
            tab_ref[c0, NZ + c] = c * tok + before[c] - start
            start = start + n
            before[c] = before[c] + n
            tab_ref[c0, c] = start

    def placed(ids, plane):
        pos = ids + tab_ref[plane, NZ]
        for c in range(1, NZ):
            pos = jnp.where(ids >= tab_ref[plane, c - 1], ids + tab_ref[plane, NZ + c], pos)
        return jnp.where(ids >= tab_ref[plane, NZ - 1], FAR, pos)

    first = lax.broadcasted_iota(jnp.int32, (1, HDIM), 1) * KS
    k_min = k_max = None
    for c0 in range(NZ):
        low, high = placed(first, c0), placed(first + (KS - 1), c0)
        k_min = low if c0 == 0 else jnp.minimum(k_min, low)
        k_max = high if c0 == 0 else jnp.maximum(k_max, high)
    for b in range(qpos_ref.shape[0]):
        pos = placed(lax.broadcasted_iota(jnp.int32, (1, QB), 1) + b * QB, z)
        lo = jnp.zeros_like(pos)
        bound = jnp.int32(0)
        for m in range(doc_ref.shape[1]):
            bound = bound + doc_ref[0, m]
            lo = jnp.where(pos >= bound, bound, lo)
        hi = jnp.where(pos < FAR, pos, -1)
        qpos_ref[b, 0:1, :] = hi
        qpos_ref[b, 1:2, :] = lo
        q_max = jnp.max(hi.astype(F32)).astype(jnp.int32)
        q_min = jnp.min(jnp.where(pos < FAR, lo, FAR).astype(F32)).astype(jnp.int32)
        span_ref[0, b] = jnp.sum(jnp.where(k_max < q_min, 1.0, 0.0)).astype(jnp.int32)
        span_ref[1, b] = jnp.sum(jnp.where(k_min <= q_max, 1.0, 0.0)).astype(jnp.int32)


def tables(route_counts, doc_lengths, tok):
    blocks = -(-SLOW[0] // QB)
    i32 = jnp.int32
    return pl.pallas_call(
        functools.partial(tables_kernel, tok),
        out_shape=(
            jax.ShapeDtypeStruct((1, tok), i32), jax.ShapeDtypeStruct((1, ND * SLOW[1]), i32),
            jax.ShapeDtypeStruct((blocks, 2, QB), i32), jax.ShapeDtypeStruct((NZ, 2 * NZ), i32),
            jax.ShapeDtypeStruct((2, blocks), i32), jax.ShapeDtypeStruct((1,), i32),
        ),
        in_specs=[SMEM_SPEC, VMEM_SPEC, SMEM_SPEC],
        out_specs=(VMEM_SPEC,) * 3 + (SMEM_SPEC,) * 3,
        scratch_shapes=[pltpu.SMEM((ND, NZ), i32)],
        name="routing_tables",
    )(route_counts, route_counts, doc_lengths)


def greet():
    z = lax.axis_index("ctx")
    d = lax.axis_index("dp")
    barrier = pltpu.get_barrier_semaphore()
    for s in range(1, ND):
        pl.semaphore_signal(barrier, inc=1, device_id={"dp": lax.rem(d + s, ND)}, device_id_type=MESH)
    for s in (1, NZ - 1):
        pl.semaphore_signal(barrier, inc=1, device_id={"ctx": lax.rem(z + s, NZ)}, device_id_type=MESH)
    pl.semaphore_wait(barrier, ND + 1)


def exchange(src, dst, send, recv):
    d = lax.axis_index("dp")
    copies = []
    for s in range(1, ND):
        to = lax.rem(d + s, ND)
        copies.append(pltpu.make_async_remote_copy(
            src_ref=src.at[to], dst_ref=dst.at[d], send_sem=send.at[s], recv_sem=recv.at[s],
            device_id={"dp": to}, device_id_type=MESH))
    return copies


def along(axis_by, src, dst, send, recv):
    z = lax.axis_index("ctx")
    return pltpu.make_async_remote_copy(
        src_ref=src, dst_ref=dst, send_sem=send, recv_sem=recv,
        device_id={"ctx": lax.rem(z + axis_by, NZ)}, device_id_type=MESH)


def dispatch_kernel(q_ref, k_ref, v_ref, o_ref, g_ref, l_ref, slot_ref, idx_ref, all_ref, rq_ref, rg_ref,
                    qv, kv, vv, ov, gv, stat, sk, sv, sq, sg, rk, rv, mine,
                    ins, ks, kr, vs, vr, qs, qr, gs, gr, ls, fs, fr, bs, br):
    z = lax.axis_index("ctx")
    d = lax.axis_index("dp")
    width = qv.shape[1]
    heads = width // HDIM
    kvw = k_ref.shape[1]
    slots, pair = sk.shape[0] * sk.shape[1], sk.shape[1]
    cap = mine.shape[0]
    loads = []
    for n, (src, dst) in enumerate(((k_ref, kv), (v_ref, vv), (q_ref, qv), (g_ref, gv), (o_ref, ov))):
        c = pltpu.make_async_copy(src, dst, ins.at[n])
        c.start()
        loads.append(c)
    greet()
    pick = one_hot_rows(slots, slot_ref[...])
    kv_copies = []
    own = []
    for n, (src, out, into, send, recv) in enumerate(((kv, sk, rk, ks, kr), (vv, sv, rv, vs, vr))):
        loads[n].wait()
        out[...] = dot(pick, src[...]).astype(BF).reshape(out.shape)
        copies = exchange(out, into, send, recv)
        for c in copies:
            c.start()
        kv_copies.append(copies)
        own.append(pltpu.make_async_copy(out.at[d], into.at[d], ls.at[n]))
        own[n].start()
    loads[2].wait()
    for at in range(0, width, 2 * HDIM):
        at = slice(at, at + 2 * HDIM)
        sq[:, :, at] = dot(pick, qv[:, at]).astype(BF).reshape(ND, pair, 2 * HDIM)
    q_copies = exchange(sq, rq_ref, qs, qr)
    for c in q_copies:
        c.start()
    own.append(pltpu.make_async_copy(sq.at[d], rq_ref.at[d], ls.at[2]))
    own[2].start()
    loads[3].wait()
    loads[4].wait()
    stat[...] = jnp.zeros_like(stat)
    for h in range(heads):
        at = slice(h * HDIM, (h + 1) * HDIM)
        both = gv[:, at].astype(F32) * ov[:, at].astype(F32)
        stat[:, h:h + 1] = jnp.sum(both, axis=1, keepdims=True)
    for at in range(0, width, 2 * HDIM):
        at = slice(at, at + 2 * HDIM)
        sg[:, :, at] = dot(pick, gv[:, at]).astype(BF).reshape(ND, pair, 2 * HDIM)
    sg[:, :, width:] = dot(pick, stat[...].astype(BF)).astype(BF).reshape(ND, pair, HDIM)
    lse = lax.dot_general(pick, l_ref[...], (((1,), (1,)), ((), ())), preferred_element_type=F32)
    sg[:, :, width + heads:width + 2 * heads] = lse.astype(BF).reshape(ND, pair, heads)
    g_copies = exchange(sg, rg_ref, gs, gr)
    for c in g_copies:
        c.start()
    own.append(pltpu.make_async_copy(sg.at[d], rg_ref.at[d], ls.at[3]))
    own[3].start()
    sent = []

    def hop(step, piece):
        cols = pl.ds(piece * kvw, kvw)
        for by, origin, send, recv, half in (
                (1, lax.rem(z - step + NZ, NZ), fs, fr, 0), (NZ - 1, lax.rem(z + step, NZ), bs, br, 1)):
            if step == NZ // 2 - 1 and piece != half:
                continue
            src = mine.at[:, cols] if step == 0 else all_ref.at[origin, :, cols]
            c = along(by, src, all_ref.at[origin, :, cols], send.at[step, piece], recv.at[step, piece])
            c.start()
            sent.append((step, piece, c))

    gather = one_hot_rows(cap, idx_ref[:, :slots])
    for piece, into in enumerate((rk, rv)):
        own[piece].wait()
        for c in kv_copies[piece]:
            c.wait_recv()
        mine[:, piece * kvw:(piece + 1) * kvw] = dot(gather, into[...].reshape(slots, kvw)).astype(BF)
        hop(0, piece)
    own.append(pltpu.make_async_copy(mine, all_ref.at[z], ls.at[4]))
    own[4].start()
    for step in range(1, NZ // 2):
        for piece in range(2):
            for s, p, c in list(sent):
                if s == step - 1 and p == piece:
                    c.wait_recv()
            hop(step, piece)
    for s, p, c in sent:
        if s == NZ // 2 - 1:
            c.wait_recv()
        c.wait_send()
    for c in kv_copies[0] + kv_copies[1]:
        c.wait_send()
    for c in q_copies + g_copies:
        c.wait()
    for c in own[2:]:
        c.wait()


def dispatch(query, keys, values, output, grad_out, log_norm, slot_row, idx_row, cap, pair, cid):
    tok, width = query.shape
    kvw = 2 * keys.shape[1]
    gw = width + HDIM
    dma = pltpu.SemaphoreType.DMA
    return pl.pallas_call(
        dispatch_kernel,
        out_shape=(
            jax.ShapeDtypeStruct((NZ, cap, kvw), BF),
            jax.ShapeDtypeStruct((ND, pair, width), BF),
            jax.ShapeDtypeStruct((ND, pair, gw), BF),
        ),
        in_specs=[ANY_SPEC] * 5 + [VMEM_SPEC] * 3,
        out_specs=(ANY_SPEC,) * 3,
        scratch_shapes=[
            pltpu.VMEM((tok, width), BF), pltpu.VMEM((tok, kvw // 2), BF), pltpu.VMEM((tok, kvw // 2), BF),
            pltpu.VMEM((tok, width), BF), pltpu.VMEM((tok, width), BF), pltpu.VMEM((tok, HDIM), F32),
            pltpu.VMEM((ND, pair, kvw // 2), BF), pltpu.VMEM((ND, pair, kvw // 2), BF),
            pltpu.VMEM((ND, pair, width), BF), pltpu.VMEM((ND, pair, gw), BF),
            pltpu.VMEM((ND, pair, kvw // 2), BF), pltpu.VMEM((ND, pair, kvw // 2), BF), pltpu.VMEM((cap, kvw), BF),
            dma((5,)), dma((ND,)), dma((ND,)), dma((ND,)), dma((ND,)), dma((ND,)), dma((ND,)),
            dma((ND,)), dma((ND,)), dma((5,)),
            dma((4, 2)), dma((4, 2)), dma((4, 2)), dma((4, 2)),
        ],
        compiler_params=pltpu.CompilerParams(
            collective_id=cid, has_side_effects=True, vmem_limit_bytes=56 << 20),
        name="dispatch_rows",
    )(query, keys, values, output, grad_out, log_norm.T, slot_row, idx_row)


def attend_kernel(group, kvh, span_ref, tab_ref, all_hbm, rq_hbm, rg_hbm, row_ref, qpos_ref, dkv_hbm, dq_hbm,
                  all_ref, rq_ref, rg_ref, qs, gs, lse, dlt, dq, dkv, kpos, dkv_ref, dq_ref, probs, dscore, order, ins):
    nq = qs.shape[1]
    capq = nq * QB
    heads = group * kvh
    width = heads * HDIM
    kvw = kvh * HDIM
    scale = HDIM ** -0.5
    cap = all_ref.shape[1]
    tile = NZ * KS
    loads = []
    for n, (src, dst) in enumerate(((rq_hbm, rq_ref), (rg_hbm, rg_ref), (all_hbm, all_ref))):
        c = pltpu.make_async_copy(src, dst, ins.at[n])
        c.start()
        loads.append(c)
    pick = one_hot_rows(capq, row_ref[:, :rq_ref.shape[0]])
    ids = lax.broadcasted_iota(jnp.int32, (cap, HDIM), 0)
    for z in range(NZ):
        p = ids + tab_ref[z, NZ]
        for c in range(NZ):
            jump = tab_ref[z, NZ + c + 1] - tab_ref[z, NZ + c] if c + 1 < NZ else FAR
            p = p + jnp.where(ids >= tab_ref[z, c], jump, 0)
        kpos[z] = p
    dq[...] = jnp.zeros_like(dq)
    dkv[...] = jnp.zeros_like(dkv)
    for load, src, dst in ((loads[0], rq_ref, qs), (loads[1], rg_ref, gs)):
        load.wait()
        for h in range(0, heads, 2):
            both = dot(pick, src[:, h * HDIM:(h + 2) * HDIM]).astype(BF)
            for e in range(2):
                g, r = divmod(h + e, group)
                for i in range(nq):
                    dst[g, i, r * QB:(r + 1) * QB, :] = both[i * QB:(i + 1) * QB, e * HDIM:(e + 1) * HDIM]
    stat = lax.dot_general(rg_ref[:, width:], pick, (((0,), (1,)), ((), ())), preferred_element_type=F32)
    for h in range(heads):
        g, r = divmod(h, group)
        for i in range(nq):
            at = slice(i * QB, (i + 1) * QB)
            to = slice(r * QB, (r + 1) * QB)
            dlt[g, i, :, to] = jnp.broadcast_to(stat[h:h + 1, at], (8, QB))
            lse[g, i, :, to] = jnp.broadcast_to(stat[heads + h:heads + h + 1, at] * LOG2E, (8, QB))
    loads[2].wait()

    def tile_rows(t):
        return pl.ds(pl.multiple_of(t * KS, KS), KS)

    def weigh(n):
        i, slot = order[0, n], n % 2
        rows = tile_rows(order[1, n])
        kp = kpos[:, rows, :].reshape(tile, HDIM)
        seen = (kp <= qpos_ref[i, 0:1, :]) & (kp >= qpos_ref[i, 1:2, :])
        last = (((1,), (1,)), ((), ()))
        for g in range(kvh):
            kt = all_ref[:, rows, g * HDIM:(g + 1) * HDIM].reshape(tile, HDIM)
            vt = all_ref[:, rows, kvw + g * HDIM:kvw + (g + 1) * HDIM].reshape(tile, HDIM)
            s = lax.dot_general(kt, qs[g, i], last, preferred_element_type=F32)
            dp = lax.dot_general(vt, gs[g, i], last, preferred_element_type=F32)
            e = jnp.exp2(s * (scale * LOG2E) - lse[g, i, 0:1, :])
            p = jnp.concatenate(
                [jnp.where(seen, e[:, r * QB:(r + 1) * QB], 0.0) for r in range(group)], axis=1)
            probs[slot, g] = p.astype(BF)
            dscore[slot, g] = (p * (dp - dlt[g, i, 0:1, :]) * scale).astype(BF)

    def add_up(n):
        i, slot = order[0, n], n % 2
        rows = tile_rows(order[1, n])
        for g in range(kvh):
            kc = slice(g * HDIM, (g + 1) * HDIM)
            vc = slice(kvw + g * HDIM, kvw + (g + 1) * HDIM)
            ds = dscore[slot, g]
            dkv[:, rows, vc] += dot(probs[slot, g], gs[g, i]).reshape(NZ, KS, HDIM)
            dkv[:, rows, kc] += dot(ds, qs[g, i]).reshape(NZ, KS, HDIM)
            dq[g, i] += dot_rows(ds, all_ref[:, rows, kc].reshape(tile, HDIM))

    def list_block(i, n):
        def list_tile(t, n):
            order[0, n] = i
            order[1, n] = t
            return n + 1

        return lax.fori_loop(span_ref[0, i], span_ref[1, i], list_tile, n)

    total = lax.fori_loop(0, nq, list_block, jnp.int32(0))

    @pl.when(total > 0)
    def _():
        weigh(0)

    def step(n, _):
        add_up(n)
        weigh(jnp.minimum(n + 1, total))
        return 0

    order[0, total] = 0
    order[1, total] = 0
    lax.fori_loop(0, total, step, 0)
    dkv_ref[...] = dkv[...].astype(BF)
    outs = [pltpu.make_async_copy(dkv_ref, dkv_hbm, ins.at[3])]
    outs[0].start()
    back = pick.T
    for h in range(0, heads, 2):
        cols = []
        for e in range(2):
            g, r = divmod(h + e, group)
            cols.append(jnp.concatenate([dq[g, i, r * QB:(r + 1) * QB, :] for i in range(nq)], axis=0).astype(BF))
        dq_ref[:, h * HDIM:(h + 2) * HDIM] = dot(back, jnp.concatenate(cols, axis=1)).astype(BF)
    outs.append(pltpu.make_async_copy(dq_ref, dq_hbm, ins.at[4]))
    outs[1].start()
    for c in outs:
        c.wait()


def attend(span, tab, kv_all, rq, rg, idx_row, qpos, group, kvh):
    cap, kvw = kv_all.shape[1:]
    nq = -(-cap // QB)
    slots, width = rq.shape
    return pl.pallas_call(
        functools.partial(attend_kernel, group, kvh),
        out_shape=(
            jax.ShapeDtypeStruct((NZ, cap, kvw), BF),
            jax.ShapeDtypeStruct((slots, width), BF),
        ),
        in_specs=[SMEM_SPEC] * 2 + [ANY_SPEC] * 3 + [VMEM_SPEC] * 2,
        out_specs=(ANY_SPEC, ANY_SPEC),
        scratch_shapes=[
            pltpu.VMEM((NZ, cap, kvw), BF), pltpu.VMEM(rq.shape, BF), pltpu.VMEM(rg.shape, BF),
            pltpu.VMEM((kvh, nq, group * QB, HDIM), BF), pltpu.VMEM((kvh, nq, group * QB, HDIM), BF),
            pltpu.VMEM((kvh, nq, 8, group * QB), F32), pltpu.VMEM((kvh, nq, 8, group * QB), F32),
            pltpu.VMEM((kvh, nq, group * QB, HDIM), F32), pltpu.VMEM((NZ, cap, kvw), F32),
            pltpu.VMEM((NZ, cap, HDIM), jnp.int32),
            pltpu.VMEM((NZ, cap, kvw), BF), pltpu.VMEM((slots, width), BF),
            pltpu.VMEM((2, kvh, NZ * KS, group * QB), BF), pltpu.VMEM((2, kvh, NZ * KS, group * QB), BF),
            pltpu.SMEM((2, nq * (cap // KS) + 1), jnp.int32),
            pltpu.SemaphoreType.DMA((5,)),
        ],
        compiler_params=pltpu.CompilerParams(vmem_limit_bytes=60 << 20),
        name="attention_grads",
    )(span, tab, kv_all, rq, rg, idx_row, qpos)


def return_kernel(dkv_hbm, dq_ref, idx_ref, slot_ref, gq_ref, gk_ref, gv_ref,
                  dkv_ref, fin, bin_, fout, bout, sk, sv, rdq_ref, rk, rv, gq, gk, gv,
                  qs, qr, ks, kr, vs, vr, ls, fs, fr, bs, br):
    z = lax.axis_index("ctx")
    d = lax.axis_index("dp")
    cap, kvw = dkv_ref.shape[1:]
    half_w = kvw // 2
    last = NZ // 2 - 1
    load = pltpu.make_async_copy(dkv_hbm, dkv_ref, ls.at[2])
    load.start()
    greet()
    sent = []

    def hop(step, piece):
        cols = pl.ds(piece * half_w, half_w)
        for by, owner, send, recv, into, out, half in (
                (1, lax.rem(z + NZ // 2 - step, NZ), fs, fr, fin, fout, 0),
                (NZ - 1, lax.rem(z + NZ // 2 + step, NZ), bs, br, bin_, bout, 1)):
            if step == 0 and piece != half:
                continue
            if step == 0 or (step == 1 and piece != half):
                src = dkv_hbm.at[owner, :, cols]
            else:
                for s, p, b, c in sent:
                    if s == step - 1 and p == piece and b == by:
                        c.wait_recv()
                out[step, :, cols] = (dkv_ref[owner, :, cols].astype(F32)
                                      + into[step - 1, :, cols].astype(F32)).astype(BF)
                src = out.at[step, :, cols]
            c = along(by, src, into.at[step, :, cols], send.at[step, piece], recv.at[step, piece])
            c.start()
            sent.append((step, piece, by, c))

    hop(0, 0)
    hop(0, 1)
    dq_copies = exchange(dq_ref, rdq_ref, qs, qr)
    for c in dq_copies:
        c.start()
    own = pltpu.make_async_copy(dq_ref.at[d], rdq_ref.at[d], ls.at[0])
    own.start()
    load.wait()
    for step in range(1, NZ // 2):
        hop(step, 0)
        hop(step, 1)
    own.wait()
    for c in dq_copies:
        c.wait()
    count, width = sk.shape[0] * sk.shape[1], gq.shape[1]
    pick = one_hot_rows(count, slot_ref[...]).T
    rows = rdq_ref[...].reshape(count, width)
    gq[...] = dot(pick, rows).astype(BF)
    outs = [pltpu.make_async_copy(gq, gq_ref, ls.at[3])]
    outs[0].start()
    spread = one_hot_rows(cap, idx_ref[:, :count])
    returns = []
    for piece, (out, into, send, recv) in enumerate(((sk, rk, ks, kr), (sv, rv, vs, vr))):
        cols = slice(piece * half_w, (piece + 1) * half_w)
        for s, p, b, c in sent:
            if s == last and p == piece:
                c.wait_recv()
        total = (dkv_ref[z, :, cols].astype(F32) + fin[last, :, cols].astype(F32)
                 + bin_[last, :, cols].astype(F32)).astype(BF)
        out[...] = dot_rows(spread, total).astype(BF).reshape(out.shape)
        copies = exchange(out, into, send, recv)
        for c in copies:
            c.start()
        keep = pltpu.make_async_copy(out.at[d], into.at[d], ls.at[1 + 3 * piece])
        keep.start()
        returns.append(copies + [keep])
    for s, p, b, c in sent:
        c.wait_send()
    for piece, (into, stage, dst) in enumerate(((rk, gk, gk_ref), (rv, gv, gv_ref))):
        for c in returns[piece]:
            c.wait()
        stage[...] = dot(pick, into[...].reshape(count, half_w)).astype(BF)
        outs.append(pltpu.make_async_copy(stage, dst, ls.at[5 + piece]))
        outs[-1].start()
    for c in outs:
        c.wait()


def send_back(dkv, dq, idx_row, slot_row, cid):
    cap, kvw = dkv.shape[1:]
    pair, width = dq.shape[1:]
    tok = slot_row.shape[1]
    dma = pltpu.SemaphoreType.DMA
    return pl.pallas_call(
        return_kernel,
        out_shape=(
            jax.ShapeDtypeStruct((tok, width), BF),
            jax.ShapeDtypeStruct((tok, kvw // 2), BF),
            jax.ShapeDtypeStruct((tok, kvw // 2), BF),
        ),
        in_specs=[ANY_SPEC, ANY_SPEC, VMEM_SPEC, VMEM_SPEC],
        out_specs=(ANY_SPEC,) * 3,
        scratch_shapes=[pltpu.VMEM((NZ, cap, kvw), BF)] + [pltpu.VMEM((NZ // 2, cap, kvw), BF)] * 4 + [
            pltpu.VMEM((ND, pair, kvw // 2), BF), pltpu.VMEM((ND, pair, kvw // 2), BF),
            pltpu.VMEM((ND, pair, width), BF),
            pltpu.VMEM((ND, pair, kvw // 2), BF), pltpu.VMEM((ND, pair, kvw // 2), BF),
            pltpu.VMEM((tok, width), BF), pltpu.VMEM((tok, kvw // 2), BF), pltpu.VMEM((tok, kvw // 2), BF),
            dma((ND,)), dma((ND,)), dma((ND,)), dma((ND,)), dma((ND,)), dma((ND,)), dma((7,)),
            dma((4, 2)), dma((4, 2)), dma((4, 2)), dma((4, 2)),
        ],
        compiler_params=pltpu.CompilerParams(
            collective_id=cid, has_side_effects=True, vmem_limit_bytes=56 << 20),
        name="return_rows",
    )(dkv, dq, idx_row, slot_row)


def body(query, keys, values, output, grad_out, log_norm, route_counts, doc_lengths):
    tok = query.shape[0]
    kvh = keys.shape[1] // HDIM
    group = query.shape[1] // keys.shape[1]
    slot, idx, qpos, tab, span, fits = tables(route_counts, doc_lengths, tok)

    def run(size, cid, *rows):
        cap, pair = size
        slots = ND * pair
        kv_all, rq, rg = dispatch(*rows, slot, idx, cap, pair, cid)
        dkv, dq = attend(span, tab, kv_all, rq.reshape(slots, -1), rg.reshape(slots, -1), idx, qpos, group, kvh)
        return send_back(dkv, dq.reshape(ND, pair, -1), idx, slot, cid + 1)

    return lax.cond(fits[0] > 0, functools.partial(run, FAST, 0), functools.partial(run, SLOW, 2),
                    query, keys, values, output, grad_out, log_norm)


def solution(mesh):
    rows = P(("ctx", "dp"), "head")
    return jax.shard_map(
        body, mesh=mesh, in_specs=(rows,) * 6 + (P(), P("dp", None)), out_specs=(rows,) * 3, check_vma=False)
```

```python
import functools

import jax
import jax.numpy as jnp
from jax import lax
from jax.experimental import pallas as pl
from jax.experimental.pallas import tpu as pltpu
from jax.sharding import PartitionSpec as P

HDIM = 128
NZ = 8
ND = 8
QB = 128
KS = 32
FAST = (448, 80)
SLOW = (704, 88)
FAR = 1 << 20
LOG2E = 1.4426950408889634
CROSS_FIRST = (6, 5, 7, 4, 2, 1, 3)
MESH = pl.DeviceIdType.MESH
BF = jnp.bfloat16
F32 = jnp.float32
VMEM_SPEC = pl.BlockSpec(memory_space=pltpu.VMEM)
SMEM_SPEC = pl.BlockSpec(memory_space=pltpu.SMEM)
ANY_SPEC = pl.BlockSpec(memory_space=pl.ANY)


def dot(a, b):
    return jnp.dot(a, b, preferred_element_type=F32)


def one_hot_rows(count, row):
    ids = lax.broadcasted_iota(jnp.int32, (count, row.shape[1]), 0)
    return jnp.where(ids == row, 1.0, 0.0).astype(BF)


def dot_rows(a, b):
    return lax.dot_general(a, b, (((0,), (0,)), ((), ())), preferred_element_type=F32)


def tables_kernel(tok, rc_ref, counts_ref, doc_ref, slot_ref, idx_ref, qpos_ref, tab_ref, span_ref, fits_ref, tops):
    z = lax.axis_index("ctx")
    d = lax.axis_index("dp")
    owners = NZ * ND
    part_of = lax.broadcasted_iota(jnp.int32, (owners, HDIM), 0) % ND
    lanes = lax.broadcasted_iota(jnp.int32, (owners, HDIM), 1)
    pairs = dot(counts_ref[...].astype(F32).astype(BF), jnp.where(part_of == lanes, 1.0, 0.0).astype(BF))
    plane = lax.broadcasted_iota(jnp.int32, (NZ, owners), 1) // ND
    loads = dot(jnp.where(plane == lax.broadcasted_iota(jnp.int32, (NZ, owners), 0), 1.0, 0.0).astype(BF),
                pairs.astype(BF))
    fits = (jnp.max(loads) <= FAST[0]) & (jnp.max(pairs) <= FAST[1])
    fits_ref[0] = fits.astype(jnp.int32)
    pair = jnp.where(fits, FAST[1], SLOW[1])

    ids = lax.broadcasted_iota(jnp.int32, (1, tok), 1)
    slot = ids
    start = jnp.int32(0)
    filled = [jnp.int32(0)] * ND
    for f in range(owners):
        n = rc_ref[z * ND + d, f]
        to = f % ND
        slot = jnp.where(ids >= start, ids + (to * pair + filled[to] - start), slot)
        filled[to] = filled[to] + n
        start = start + n
    slot_ref[...] = slot

    start = jnp.int32(0)
    for c in range(NZ):
        for e in range(ND):
            tops[e, c] = start
            start = start + rc_ref[z * ND + e, c * ND + d]
    ids = lax.broadcasted_iota(jnp.int32, idx_ref.shape, 1)
    idx = ids
    for e in range(ND):
        start = e * pair
        for c in range(NZ):
            idx = jnp.where(ids >= start, ids + (tops[e, c] - start), idx)
            start = start + rc_ref[z * ND + e, c * ND + d]
        idx = jnp.where(ids >= start, -1, idx)
    idx_ref[...] = idx

    before = [jnp.int32(0)] * NZ
    for c0 in range(NZ):
        start = jnp.int32(0)
        for c in range(NZ):
            n = rc_ref[c0 * ND, c * ND + d]
            for e in range(1, ND):
                n = n + rc_ref[c0 * ND + e, c * ND + d]
            tab_ref[c0, NZ + c] = c * tok + before[c] - start
            start = start + n
            before[c] = before[c] + n
            tab_ref[c0, c] = start

    def placed(ids, plane):
        pos = ids + tab_ref[plane, NZ]
        for c in range(1, NZ):
            pos = jnp.where(ids >= tab_ref[plane, c - 1], ids + tab_ref[plane, NZ + c], pos)
        return jnp.where(ids >= tab_ref[plane, NZ - 1], FAR, pos)

    first = lax.broadcasted_iota(jnp.int32, (1, HDIM), 1) * KS
    k_min = k_max = None
    for c0 in range(NZ):
        low, high = placed(first, c0), placed(first + (KS - 1), c0)
        k_min = low if c0 == 0 else jnp.minimum(k_min, low)
        k_max = high if c0 == 0 else jnp.maximum(k_max, high)
    for b in range(qpos_ref.shape[0]):
        pos = placed(lax.broadcasted_iota(jnp.int32, (1, QB), 1) + b * QB, z)
        lo = jnp.zeros_like(pos)
        bound = jnp.int32(0)
        for m in range(doc_ref.shape[1]):
            bound = bound + doc_ref[0, m]
            lo = jnp.where(pos >= bound, bound, lo)
        hi = jnp.where(pos < FAR, pos, -1)
        qpos_ref[b, 0:1, :] = hi
        qpos_ref[b, 1:2, :] = lo
        q_max = jnp.max(hi.astype(F32)).astype(jnp.int32)
        q_min = jnp.min(jnp.where(pos < FAR, lo, FAR).astype(F32)).astype(jnp.int32)
        span_ref[0, b] = jnp.sum(jnp.where(k_max < q_min, 1.0, 0.0)).astype(jnp.int32)
        span_ref[1, b] = jnp.sum(jnp.where(k_min <= q_max, 1.0, 0.0)).astype(jnp.int32)


def tables(route_counts, doc_lengths, tok):
    blocks = -(-SLOW[0] // QB)
    i32 = jnp.int32
    return pl.pallas_call(
        functools.partial(tables_kernel, tok),
        out_shape=(
            jax.ShapeDtypeStruct((1, tok), i32), jax.ShapeDtypeStruct((1, ND * SLOW[1]), i32),
            jax.ShapeDtypeStruct((blocks, 2, QB), i32), jax.ShapeDtypeStruct((NZ, 2 * NZ), i32),
            jax.ShapeDtypeStruct((2, blocks), i32), jax.ShapeDtypeStruct((1,), i32),
        ),
        in_specs=[SMEM_SPEC, VMEM_SPEC, SMEM_SPEC],
        out_specs=(VMEM_SPEC,) * 3 + (SMEM_SPEC,) * 3,
        scratch_shapes=[pltpu.SMEM((ND, NZ), i32)],
        name="routing_tables",
    )(route_counts, route_counts, doc_lengths)


def greet():
    z = lax.axis_index("ctx")
    d = lax.axis_index("dp")
    barrier = pltpu.get_barrier_semaphore()
    for s in range(1, ND):
        pl.semaphore_signal(barrier, inc=1, device_id={"dp": lax.rem(d + s, ND)}, device_id_type=MESH)
    for s in (1, NZ - 1):
        pl.semaphore_signal(barrier, inc=1, device_id={"ctx": lax.rem(z + s, NZ)}, device_id_type=MESH)
    pl.semaphore_wait(barrier, ND + 1)


def exchange(src, dst, send, recv):
    d = lax.axis_index("dp")
    copies = []
    for s in CROSS_FIRST:
        to = lax.rem(d // 4 + s // 4, 2) * 4 + lax.rem(d + s, 4)
        copies.append(pltpu.make_async_remote_copy(
            src_ref=src.at[to], dst_ref=dst.at[d], send_sem=send.at[s], recv_sem=recv.at[s],
            device_id={"dp": to}, device_id_type=MESH))
    return copies


def along(axis_by, src, dst, send, recv):
    z = lax.axis_index("ctx")
    return pltpu.make_async_remote_copy(
        src_ref=src, dst_ref=dst, send_sem=send, recv_sem=recv,
        device_id={"ctx": lax.rem(z + axis_by, NZ)}, device_id_type=MESH)


def dispatch_kernel(q_ref, k_ref, v_ref, o_ref, g_ref, l_ref, slot_ref, idx_ref, all_ref, rq_ref, rg_ref,
                    qv, kv, vv, ov, gv, stat, sk, sv, sq, sg, rk, rv, mine,
                    ins, ks, kr, vs, vr, qs, qr, gs, gr, ls, fs, fr, bs, br):
    z = lax.axis_index("ctx")
    d = lax.axis_index("dp")
    width = qv.shape[1]
    heads = width // HDIM
    kvw = k_ref.shape[1]
    slots, pair = sk.shape[0] * sk.shape[1], sk.shape[1]
    cap = mine.shape[0]
    loads = []
    for n, (src, dst) in enumerate(((k_ref, kv), (v_ref, vv), (q_ref, qv), (g_ref, gv), (o_ref, ov))):
        c = pltpu.make_async_copy(src, dst, ins.at[n])
        c.start()
        loads.append(c)
    greet()
    pick = one_hot_rows(slots, slot_ref[...])
    kv_copies = []
    own = []
    for n, (src, out, into, send, recv) in enumerate(((kv, sk, rk, ks, kr), (vv, sv, rv, vs, vr))):
        loads[n].wait()
        out[...] = dot(pick, src[...]).astype(BF).reshape(out.shape)
        copies = exchange(out, into, send, recv)
        for c in copies:
            c.start()
        kv_copies.append(copies)
        own.append(pltpu.make_async_copy(out.at[d], into.at[d], ls.at[n]))
        own[n].start()
    loads[2].wait()
    for at in range(0, width, 2 * HDIM):
        at = slice(at, at + 2 * HDIM)
        sq[:, :, at] = dot(pick, qv[:, at]).astype(BF).reshape(ND, pair, 2 * HDIM)
    q_copies = exchange(sq, rq_ref, qs, qr)
    for c in q_copies:
        c.start()
    own.append(pltpu.make_async_copy(sq.at[d], rq_ref.at[d], ls.at[2]))
    own[2].start()
    loads[3].wait()
    loads[4].wait()
    stat[...] = jnp.zeros_like(stat)
    for h in range(heads):
        at = slice(h * HDIM, (h + 1) * HDIM)
        both = gv[:, at].astype(F32) * ov[:, at].astype(F32)
        stat[:, h:h + 1] = jnp.sum(both, axis=1, keepdims=True)
    for at in range(0, width, 2 * HDIM):
        at = slice(at, at + 2 * HDIM)
        sg[:, :, at] = dot(pick, gv[:, at]).astype(BF).reshape(ND, pair, 2 * HDIM)
    sg[:, :, width:] = dot(pick, stat[...].astype(BF)).astype(BF).reshape(ND, pair, HDIM)
    lse = lax.dot_general(pick, l_ref[...], (((1,), (1,)), ((), ())), preferred_element_type=F32)
    sg[:, :, width + heads:width + 2 * heads] = lse.astype(BF).reshape(ND, pair, heads)
    g_copies = exchange(sg, rg_ref, gs, gr)
    for c in g_copies:
        c.start()
    own.append(pltpu.make_async_copy(sg.at[d], rg_ref.at[d], ls.at[3]))
    own[3].start()
    sent = []

    def hop(step, piece):
        cols = pl.ds(piece * kvw, kvw)
        for by, origin, send, recv, half in (
                (1, lax.rem(z - step + NZ, NZ), fs, fr, 0), (NZ - 1, lax.rem(z + step, NZ), bs, br, 1)):
            if step == NZ // 2 - 1 and piece != half:
                continue
            src = mine.at[:, cols] if step == 0 else all_ref.at[origin, :, cols]
            c = along(by, src, all_ref.at[origin, :, cols], send.at[step, piece], recv.at[step, piece])
            c.start()
            sent.append((step, piece, c))

    gather = one_hot_rows(cap, idx_ref[:, :slots])
    for piece, into in enumerate((rk, rv)):
        own[piece].wait()
        for c in kv_copies[piece]:
            c.wait_recv()
        mine[:, piece * kvw:(piece + 1) * kvw] = dot(gather, into[...].reshape(slots, kvw)).astype(BF)
        hop(0, piece)
    own.append(pltpu.make_async_copy(mine, all_ref.at[z], ls.at[4]))
    own[4].start()
    for step in range(1, NZ // 2):
        for piece in range(2):
            for s, p, c in list(sent):
                if s == step - 1 and p == piece:
                    c.wait_recv()
            hop(step, piece)
    for s, p, c in sent:
        if s == NZ // 2 - 1:
            c.wait_recv()
        c.wait_send()
    for c in kv_copies[0] + kv_copies[1]:
        c.wait_send()
    for c in q_copies + g_copies:
        c.wait()
    for c in own[2:]:
        c.wait()


def dispatch(query, keys, values, output, grad_out, log_norm, slot_row, idx_row, cap, pair, cid):
    tok, width = query.shape
    kvw = 2 * keys.shape[1]
    gw = width + HDIM
    dma = pltpu.SemaphoreType.DMA
    return pl.pallas_call(
        dispatch_kernel,
        out_shape=(
            jax.ShapeDtypeStruct((NZ, cap, kvw), BF),
            jax.ShapeDtypeStruct((ND, pair, width), BF),
            jax.ShapeDtypeStruct((ND, pair, gw), BF),
        ),
        in_specs=[ANY_SPEC] * 5 + [VMEM_SPEC] * 3,
        out_specs=(ANY_SPEC,) * 3,
        scratch_shapes=[
            pltpu.VMEM((tok, width), BF), pltpu.VMEM((tok, kvw // 2), BF), pltpu.VMEM((tok, kvw // 2), BF),
            pltpu.VMEM((tok, width), BF), pltpu.VMEM((tok, width), BF), pltpu.VMEM((tok, HDIM), F32),
            pltpu.VMEM((ND, pair, kvw // 2), BF), pltpu.VMEM((ND, pair, kvw // 2), BF),
            pltpu.VMEM((ND, pair, width), BF), pltpu.VMEM((ND, pair, gw), BF),
            pltpu.VMEM((ND, pair, kvw // 2), BF), pltpu.VMEM((ND, pair, kvw // 2), BF), pltpu.VMEM((cap, kvw), BF),
            dma((5,)), dma((ND,)), dma((ND,)), dma((ND,)), dma((ND,)), dma((ND,)), dma((ND,)),
            dma((ND,)), dma((ND,)), dma((5,)),
            dma((4, 2)), dma((4, 2)), dma((4, 2)), dma((4, 2)),
        ],
        compiler_params=pltpu.CompilerParams(
            collective_id=cid, has_side_effects=True, vmem_limit_bytes=56 << 20),
        name="dispatch_rows",
    )(query, keys, values, output, grad_out, log_norm.T, slot_row, idx_row)


def attend_kernel(group, kvh, span_ref, tab_ref, all_hbm, rq_hbm, rg_hbm, row_ref, qpos_ref, dkv_hbm, dq_hbm,
                  all_ref, rq_ref, rg_ref, qs, gs, lse, dlt, dq, dkv, kpos, dkv_ref, dq_ref, probs, dscore, order, ins):
    nq = qs.shape[1]
    capq = nq * QB
    heads = group * kvh
    width = heads * HDIM
    kvw = kvh * HDIM
    scale = HDIM ** -0.5
    cap = all_ref.shape[1]
    tile = NZ * KS
    loads = []
    for n, (src, dst) in enumerate(((rq_hbm, rq_ref), (rg_hbm, rg_ref), (all_hbm, all_ref))):
        c = pltpu.make_async_copy(src, dst, ins.at[n])
        c.start()
        loads.append(c)
    pick = one_hot_rows(capq, row_ref[:, :rq_ref.shape[0]])
    ids = lax.broadcasted_iota(jnp.int32, (cap, HDIM), 0)
    for z in range(NZ):
        p = ids + tab_ref[z, NZ]
        for c in range(NZ):
            jump = tab_ref[z, NZ + c + 1] - tab_ref[z, NZ + c] if c + 1 < NZ else FAR
            p = p + jnp.where(ids >= tab_ref[z, c], jump, 0)
        kpos[z] = p
    dq[...] = jnp.zeros_like(dq)
    dkv[...] = jnp.zeros_like(dkv)
    for load, src, dst in ((loads[0], rq_ref, qs), (loads[1], rg_ref, gs)):
        load.wait()
        for h in range(0, heads, 2):
            both = dot(pick, src[:, h * HDIM:(h + 2) * HDIM]).astype(BF)
            for e in range(2):
                g, r = divmod(h + e, group)
                for i in range(nq):
                    dst[g, i, r * QB:(r + 1) * QB, :] = both[i * QB:(i + 1) * QB, e * HDIM:(e + 1) * HDIM]
    stat = lax.dot_general(rg_ref[:, width:], pick, (((0,), (1,)), ((), ())), preferred_element_type=F32)
    for h in range(heads):
        g, r = divmod(h, group)
        for i in range(nq):
            at = slice(i * QB, (i + 1) * QB)
            to = slice(r * QB, (r + 1) * QB)
            dlt[g, i, :, to] = jnp.broadcast_to(stat[h:h + 1, at], (8, QB))
            lse[g, i, :, to] = jnp.broadcast_to(stat[heads + h:heads + h + 1, at] * LOG2E, (8, QB))
    loads[2].wait()

    def tile_rows(t):
        return pl.ds(pl.multiple_of(t * KS, KS), KS)

    def weigh(n):
        i, slot = order[0, n], n % 2
        rows = tile_rows(order[1, n])
        kp = kpos[:, rows, :].reshape(tile, HDIM)
        seen = (kp <= qpos_ref[i, 0:1, :]) & (kp >= qpos_ref[i, 1:2, :])
        last = (((1,), (1,)), ((), ()))
        for g in range(kvh):
            kt = all_ref[:, rows, g * HDIM:(g + 1) * HDIM].reshape(tile, HDIM)
            vt = all_ref[:, rows, kvw + g * HDIM:kvw + (g + 1) * HDIM].reshape(tile, HDIM)
            s = lax.dot_general(kt, qs[g, i], last, preferred_element_type=F32)
            dp = lax.dot_general(vt, gs[g, i], last, preferred_element_type=F32)
            e = jnp.exp2(s * (scale * LOG2E) - lse[g, i, 0:1, :])
            p = jnp.concatenate(
                [jnp.where(seen, e[:, r * QB:(r + 1) * QB], 0.0) for r in range(group)], axis=1)
            probs[slot, g] = p.astype(BF)
            dscore[slot, g] = (p * (dp - dlt[g, i, 0:1, :]) * scale).astype(BF)

    def add_up(n):
        i, slot = order[0, n], n % 2
        rows = tile_rows(order[1, n])
        for g in range(kvh):
            kc = slice(g * HDIM, (g + 1) * HDIM)
            vc = slice(kvw + g * HDIM, kvw + (g + 1) * HDIM)
            ds = dscore[slot, g]
            dkv[:, rows, vc] += dot(probs[slot, g], gs[g, i]).reshape(NZ, KS, HDIM)
            dkv[:, rows, kc] += dot(ds, qs[g, i]).reshape(NZ, KS, HDIM)
            dq[g, i] += dot_rows(all_ref[:, rows, kc].reshape(tile, HDIM), ds)

    def list_block(i, n):
        def list_tile(t, n):
            order[0, n] = i
            order[1, n] = t
            return n + 1

        return lax.fori_loop(span_ref[0, i], span_ref[1, i], list_tile, n)

    total = lax.fori_loop(0, nq, list_block, jnp.int32(0))

    @pl.when(total > 0)
    def _():
        weigh(0)

    def step(n, _):
        add_up(n)
        weigh(jnp.minimum(n + 1, total))
        return 0

    order[0, total] = 0
    order[1, total] = 0
    lax.fori_loop(0, total, step, 0)
    dkv_ref[...] = dkv[...].astype(BF)
    outs = [pltpu.make_async_copy(dkv_ref, dkv_hbm, ins.at[3])]
    outs[0].start()
    back = pick.T
    for h in range(0, heads, 2):
        cols = []
        for e in range(2):
            g, r = divmod(h + e, group)
            cols.append(jnp.concatenate([dq[g, i, :, r * QB:(r + 1) * QB] for i in range(nq)], axis=1).astype(BF))
        both = lax.dot_general(back, jnp.concatenate(cols, axis=0), (((1,), (1,)), ((), ())),
                               preferred_element_type=F32)
        dq_ref[:, h * HDIM:(h + 2) * HDIM] = both.astype(BF)
    outs.append(pltpu.make_async_copy(dq_ref, dq_hbm, ins.at[4]))
    outs[1].start()
    for c in outs:
        c.wait()


def attend(span, tab, kv_all, rq, rg, idx_row, qpos, group, kvh):
    cap, kvw = kv_all.shape[1:]
    nq = -(-cap // QB)
    slots, width = rq.shape
    return pl.pallas_call(
        functools.partial(attend_kernel, group, kvh),
        out_shape=(
            jax.ShapeDtypeStruct((NZ, cap, kvw), BF),
            jax.ShapeDtypeStruct((slots, width), BF),
        ),
        in_specs=[SMEM_SPEC] * 2 + [ANY_SPEC] * 3 + [VMEM_SPEC] * 2,
        out_specs=(ANY_SPEC, ANY_SPEC),
        scratch_shapes=[
            pltpu.VMEM((NZ, cap, kvw), BF), pltpu.VMEM(rq.shape, BF), pltpu.VMEM(rg.shape, BF),
            pltpu.VMEM((kvh, nq, group * QB, HDIM), BF), pltpu.VMEM((kvh, nq, group * QB, HDIM), BF),
            pltpu.VMEM((kvh, nq, 8, group * QB), F32), pltpu.VMEM((kvh, nq, 8, group * QB), F32),
            pltpu.VMEM((kvh, nq, HDIM, group * QB), F32), pltpu.VMEM((NZ, cap, kvw), F32),
            pltpu.VMEM((NZ, cap, HDIM), jnp.int32),
            pltpu.VMEM((NZ, cap, kvw), BF), pltpu.VMEM((slots, width), BF),
            pltpu.VMEM((2, kvh, NZ * KS, group * QB), BF), pltpu.VMEM((2, kvh, NZ * KS, group * QB), BF),
            pltpu.SMEM((2, nq * (cap // KS) + 1), jnp.int32),
            pltpu.SemaphoreType.DMA((5,)),
        ],
        compiler_params=pltpu.CompilerParams(vmem_limit_bytes=60 << 20),
        name="attention_grads",
    )(span, tab, kv_all, rq, rg, idx_row, qpos)


def return_kernel(dkv_hbm, dq_ref, idx_ref, slot_ref, gq_ref, gk_ref, gv_ref,
                  dkv_ref, fin, bin_, fout, bout, sk, sv, rdq_ref, rk, rv, gq, gk, gv,
                  qs, qr, ks, kr, vs, vr, ls, fs, fr, bs, br):
    z = lax.axis_index("ctx")
    d = lax.axis_index("dp")
    cap, kvw = dkv_ref.shape[1:]
    half_w = kvw // 2
    last = NZ // 2 - 1
    load = pltpu.make_async_copy(dkv_hbm, dkv_ref, ls.at[2])
    load.start()
    greet()
    sent = []

    def hop(step, piece):
        cols = pl.ds(piece * half_w, half_w)
        for by, owner, send, recv, into, out, half in (
                (1, lax.rem(z + NZ // 2 - step, NZ), fs, fr, fin, fout, 0),
                (NZ - 1, lax.rem(z + NZ // 2 + step, NZ), bs, br, bin_, bout, 1)):
            if step == 0 and piece != half:
                continue
            if step == 0 or (step == 1 and piece != half):
                src = dkv_hbm.at[owner, :, cols]
            else:
                for s, p, b, c in sent:
                    if s == step - 1 and p == piece and b == by:
                        c.wait_recv()
                out[step, :, cols] = (dkv_ref[owner, :, cols].astype(F32)
                                      + into[step - 1, :, cols].astype(F32)).astype(BF)
                src = out.at[step, :, cols]
            c = along(by, src, into.at[step, :, cols], send.at[step, piece], recv.at[step, piece])
            c.start()
            sent.append((step, piece, by, c))

    hop(0, 0)
    hop(0, 1)
    dq_copies = exchange(dq_ref, rdq_ref, qs, qr)
    for c in dq_copies:
        c.start()
    own = pltpu.make_async_copy(dq_ref.at[d], rdq_ref.at[d], ls.at[0])
    own.start()
    load.wait()
    for step in range(1, NZ // 2):
        hop(step, 0)
        hop(step, 1)
    own.wait()
    for c in dq_copies:
        c.wait()
    count, width = sk.shape[0] * sk.shape[1], gq.shape[1]
    pick = one_hot_rows(count, slot_ref[...]).T
    rows = rdq_ref[...].reshape(count, width)
    gq[...] = dot(pick, rows).astype(BF)
    outs = [pltpu.make_async_copy(gq, gq_ref, ls.at[3])]
    outs[0].start()
    spread = one_hot_rows(cap, idx_ref[:, :count])
    returns = []
    for piece, (out, into, send, recv) in enumerate(((sk, rk, ks, kr), (sv, rv, vs, vr))):
        cols = slice(piece * half_w, (piece + 1) * half_w)
        for s, p, b, c in sent:
            if s == last and p == piece:
                c.wait_recv()
        total = (dkv_ref[z, :, cols].astype(F32) + fin[last, :, cols].astype(F32)
                 + bin_[last, :, cols].astype(F32)).astype(BF)
        out[...] = dot_rows(spread, total).astype(BF).reshape(out.shape)
        copies = exchange(out, into, send, recv)
        for c in copies:
            c.start()
        keep = pltpu.make_async_copy(out.at[d], into.at[d], ls.at[1 + 3 * piece])
        keep.start()
        returns.append(copies + [keep])
    for s, p, b, c in sent:
        c.wait_send()
    for piece, (into, stage, dst) in enumerate(((rk, gk, gk_ref), (rv, gv, gv_ref))):
        for c in returns[piece]:
            c.wait()
        stage[...] = dot(pick, into[...].reshape(count, half_w)).astype(BF)
        outs.append(pltpu.make_async_copy(stage, dst, ls.at[5 + piece]))
        outs[-1].start()
    for c in outs:
        c.wait()


def send_back(dkv, dq, idx_row, slot_row, cid):
    cap, kvw = dkv.shape[1:]
    pair, width = dq.shape[1:]
    tok = slot_row.shape[1]
    dma = pltpu.SemaphoreType.DMA
    return pl.pallas_call(
        return_kernel,
        out_shape=(
            jax.ShapeDtypeStruct((tok, width), BF),
            jax.ShapeDtypeStruct((tok, kvw // 2), BF),
            jax.ShapeDtypeStruct((tok, kvw // 2), BF),
        ),
        in_specs=[ANY_SPEC, ANY_SPEC, VMEM_SPEC, VMEM_SPEC],
        out_specs=(ANY_SPEC,) * 3,
        scratch_shapes=[pltpu.VMEM((NZ, cap, kvw), BF)] + [pltpu.VMEM((NZ // 2, cap, kvw), BF)] * 4 + [
            pltpu.VMEM((ND, pair, kvw // 2), BF), pltpu.VMEM((ND, pair, kvw // 2), BF),
            pltpu.VMEM((ND, pair, width), BF),
            pltpu.VMEM((ND, pair, kvw // 2), BF), pltpu.VMEM((ND, pair, kvw // 2), BF),
            pltpu.VMEM((tok, width), BF), pltpu.VMEM((tok, kvw // 2), BF), pltpu.VMEM((tok, kvw // 2), BF),
            dma((ND,)), dma((ND,)), dma((ND,)), dma((ND,)), dma((ND,)), dma((ND,)), dma((7,)),
            dma((4, 2)), dma((4, 2)), dma((4, 2)), dma((4, 2)),
        ],
        compiler_params=pltpu.CompilerParams(
            collective_id=cid, has_side_effects=True, vmem_limit_bytes=56 << 20),
        name="return_rows",
    )(dkv, dq, idx_row, slot_row)


def body(query, keys, values, output, grad_out, log_norm, route_counts, doc_lengths):
    tok = query.shape[0]
    kvh = keys.shape[1] // HDIM
    group = query.shape[1] // keys.shape[1]
    slot, idx, qpos, tab, span, fits = tables(route_counts, doc_lengths, tok)

    def run(size, cid, *rows):
        cap, pair = size
        slots = ND * pair
        kv_all, rq, rg = dispatch(*rows, slot, idx, cap, pair, cid)
        dkv, dq = attend(span, tab, kv_all, rq.reshape(slots, -1), rg.reshape(slots, -1), idx, qpos, group, kvh)
        return send_back(dkv, dq.reshape(ND, pair, -1), idx, slot, cid + 1)

    return lax.cond(fits[0] > 0, functools.partial(run, FAST, 0), functools.partial(run, SLOW, 2),
                    query, keys, values, output, grad_out, log_norm)


def solution(mesh):
    rows = P(("ctx", "dp"), "head")
    return jax.shard_map(
        body, mesh=mesh, in_specs=(rows,) * 6 + (P(), P("dp", None)), out_specs=(rows,) * 3, check_vma=False)
```

```python
import functools

import jax
import jax.numpy as jnp
from jax import lax
from jax.experimental import pallas as pl
from jax.experimental.pallas import tpu as pltpu
from jax.sharding import PartitionSpec as P

HDIM = 128
NZ = 8
ND = 8
QB = 128
KS = 32
FAST = (448, 80)
SLOW = (704, 88)
FAR = 1 << 20
LOG2E = 1.4426950408889634
CROSS_FIRST = (6, 5, 7, 4, 2, 1, 3)
MESH = pl.DeviceIdType.MESH
BF = jnp.bfloat16
F32 = jnp.float32
VMEM_SPEC = pl.BlockSpec(memory_space=pltpu.VMEM)
SMEM_SPEC = pl.BlockSpec(memory_space=pltpu.SMEM)
ANY_SPEC = pl.BlockSpec(memory_space=pl.ANY)


def dot(a, b):
    return jnp.dot(a, b, preferred_element_type=F32)


def one_hot_rows(count, row):
    ids = lax.broadcasted_iota(jnp.int32, (count, row.shape[1]), 0)
    return jnp.where(ids == row, 1.0, 0.0).astype(BF)


def dot_rows(a, b):
    return lax.dot_general(a, b, (((0,), (0,)), ((), ())), preferred_element_type=F32)


def tables_kernel(tok, rc_ref, counts_ref, doc_ref, slot_ref, idx_ref, qpos_ref, tab_ref, span_ref, fits_ref, tops):
    z = lax.axis_index("ctx")
    d = lax.axis_index("dp")
    owners = NZ * ND
    part_of = lax.broadcasted_iota(jnp.int32, (owners, HDIM), 0) % ND
    lanes = lax.broadcasted_iota(jnp.int32, (owners, HDIM), 1)
    pairs = dot(counts_ref[...].astype(F32).astype(BF), jnp.where(part_of == lanes, 1.0, 0.0).astype(BF))
    plane = lax.broadcasted_iota(jnp.int32, (NZ, owners), 1) // ND
    loads = dot(jnp.where(plane == lax.broadcasted_iota(jnp.int32, (NZ, owners), 0), 1.0, 0.0).astype(BF),
                pairs.astype(BF))
    fits = (jnp.max(loads) <= FAST[0]) & (jnp.max(pairs) <= FAST[1])
    fits_ref[0] = fits.astype(jnp.int32)
    pair = jnp.where(fits, FAST[1], SLOW[1])

    ids = lax.broadcasted_iota(jnp.int32, (1, tok), 1)
    slot = ids
    start = jnp.int32(0)
    filled = [jnp.int32(0)] * ND
    for f in range(owners):
        n = rc_ref[z * ND + d, f]
        to = f % ND
        slot = jnp.where(ids >= start, ids + (to * pair + filled[to] - start), slot)
        filled[to] = filled[to] + n
        start = start + n
    slot_ref[...] = slot

    start = jnp.int32(0)
    for c in range(NZ):
        for e in range(ND):
            tops[e, c] = start
            start = start + rc_ref[z * ND + e, c * ND + d]
    ids = lax.broadcasted_iota(jnp.int32, idx_ref.shape, 1)
    idx = ids
    for e in range(ND):
        start = e * pair
        for c in range(NZ):
            idx = jnp.where(ids >= start, ids + (tops[e, c] - start), idx)
            start = start + rc_ref[z * ND + e, c * ND + d]
        idx = jnp.where(ids >= start, -1, idx)
    idx_ref[...] = idx

    before = [jnp.int32(0)] * NZ
    for c0 in range(NZ):
        start = jnp.int32(0)
        for c in range(NZ):
            n = rc_ref[c0 * ND, c * ND + d]
            for e in range(1, ND):
                n = n + rc_ref[c0 * ND + e, c * ND + d]
            tab_ref[c0, NZ + c] = c * tok + before[c] - start
            start = start + n
            before[c] = before[c] + n
            tab_ref[c0, c] = start

    def placed(ids, plane):
        pos = ids + tab_ref[plane, NZ]
        for c in range(1, NZ):
            pos = jnp.where(ids >= tab_ref[plane, c - 1], ids + tab_ref[plane, NZ + c], pos)
        return jnp.where(ids >= tab_ref[plane, NZ - 1], FAR, pos)

    first = lax.broadcasted_iota(jnp.int32, (1, HDIM), 1) * KS
    k_min = k_max = None
    for c0 in range(NZ):
        low, high = placed(first, c0), placed(first + (KS - 1), c0)
        k_min = low if c0 == 0 else jnp.minimum(k_min, low)
        k_max = high if c0 == 0 else jnp.maximum(k_max, high)
    for b in range(qpos_ref.shape[0]):
        pos = placed(lax.broadcasted_iota(jnp.int32, (1, QB), 1) + b * QB, z)
        lo = jnp.zeros_like(pos)
        bound = jnp.int32(0)
        for m in range(doc_ref.shape[1]):
            bound = bound + doc_ref[0, m]
            lo = jnp.where(pos >= bound, bound, lo)
        hi = jnp.where(pos < FAR, pos, -1)
        qpos_ref[b, 0:1, :] = hi
        qpos_ref[b, 1:2, :] = lo
        q_max = jnp.max(hi.astype(F32)).astype(jnp.int32)
        q_min = jnp.min(jnp.where(pos < FAR, lo, FAR).astype(F32)).astype(jnp.int32)
        span_ref[0, b] = jnp.sum(jnp.where(k_max < q_min, 1.0, 0.0)).astype(jnp.int32)
        span_ref[1, b] = jnp.sum(jnp.where(k_min <= q_max, 1.0, 0.0)).astype(jnp.int32)


def tables(route_counts, doc_lengths, tok):
    blocks = -(-SLOW[0] // QB)
    i32 = jnp.int32
    return pl.pallas_call(
        functools.partial(tables_kernel, tok),
        out_shape=(
            jax.ShapeDtypeStruct((1, tok), i32), jax.ShapeDtypeStruct((1, ND * SLOW[1]), i32),
            jax.ShapeDtypeStruct((blocks, 2, QB), i32), jax.ShapeDtypeStruct((NZ, 2 * NZ), i32),
            jax.ShapeDtypeStruct((2, blocks), i32), jax.ShapeDtypeStruct((1,), i32),
        ),
        in_specs=[SMEM_SPEC, VMEM_SPEC, SMEM_SPEC],
        out_specs=(VMEM_SPEC,) * 3 + (SMEM_SPEC,) * 3,
        scratch_shapes=[pltpu.SMEM((ND, NZ), i32)],
        name="routing_tables",
    )(route_counts, route_counts, doc_lengths)


def greet():
    z = lax.axis_index("ctx")
    d = lax.axis_index("dp")
    barrier = pltpu.get_barrier_semaphore()
    for s in range(1, ND):
        pl.semaphore_signal(barrier, inc=1, device_id={"dp": lax.rem(d + s, ND)}, device_id_type=MESH)
    for s in (1, NZ - 1):
        pl.semaphore_signal(barrier, inc=1, device_id={"ctx": lax.rem(z + s, NZ)}, device_id_type=MESH)
    pl.semaphore_wait(barrier, ND + 1)


def exchange(src, dst, send, recv):
    d = lax.axis_index("dp")
    copies = []
    for s in CROSS_FIRST:
        to = lax.rem(d // 4 + s // 4, 2) * 4 + lax.rem(d + s, 4)
        copies.append(pltpu.make_async_remote_copy(
            src_ref=src.at[to], dst_ref=dst.at[d], send_sem=send.at[s], recv_sem=recv.at[s],
            device_id={"dp": to}, device_id_type=MESH))
    return copies


def along(axis_by, src, dst, send, recv):
    z = lax.axis_index("ctx")
    return pltpu.make_async_remote_copy(
        src_ref=src, dst_ref=dst, send_sem=send, recv_sem=recv,
        device_id={"ctx": lax.rem(z + axis_by, NZ)}, device_id_type=MESH)


def dispatch_kernel(q_ref, k_ref, v_ref, o_ref, g_ref, l_ref, slot_ref, idx_ref, all_ref, rq_ref, rg_ref,
                    qv, kv, vv, ov, gv, stat, sk, sv, sq, sg, rk, rv, mine,
                    ins, ks, kr, vs, vr, qs, qr, gs, gr, ls, fs, fr, bs, br):
    z = lax.axis_index("ctx")
    d = lax.axis_index("dp")
    width = qv.shape[1]
    heads = width // HDIM
    kvw = k_ref.shape[1]
    slots, pair = sk.shape[0] * sk.shape[1], sk.shape[1]
    cap = mine.shape[0]
    loads = []
    for n, (src, dst) in enumerate(((k_ref, kv), (v_ref, vv), (q_ref, qv), (g_ref, gv), (o_ref, ov))):
        c = pltpu.make_async_copy(src, dst, ins.at[n])
        c.start()
        loads.append(c)
    greet()
    pick = one_hot_rows(slots, slot_ref[...])
    kv_copies = []
    own = []
    for n, (src, out, into, send, recv) in enumerate(((kv, sk, rk, ks, kr), (vv, sv, rv, vs, vr))):
        loads[n].wait()
        out[...] = dot(pick, src[...]).astype(BF).reshape(out.shape)
        copies = exchange(out, into, send, recv)
        for c in copies:
            c.start()
        kv_copies.append(copies)
        own.append(pltpu.make_async_copy(out.at[d], into.at[d], ls.at[n]))
        own[n].start()
    loads[2].wait()
    for at in range(0, width, 2 * HDIM):
        at = slice(at, at + 2 * HDIM)
        sq[:, :, at] = dot(pick, qv[:, at]).astype(BF).reshape(ND, pair, 2 * HDIM)
    q_copies = exchange(sq, rq_ref, qs, qr)
    for c in q_copies:
        c.start()
    own.append(pltpu.make_async_copy(sq.at[d], rq_ref.at[d], ls.at[2]))
    own[2].start()
    loads[3].wait()
    loads[4].wait()
    stat[...] = jnp.zeros_like(stat)
    for h in range(heads):
        at = slice(h * HDIM, (h + 1) * HDIM)
        both = gv[:, at].astype(F32) * ov[:, at].astype(F32)
        stat[:, h:h + 1] = jnp.sum(both, axis=1, keepdims=True)
    for at in range(0, width, 2 * HDIM):
        at = slice(at, at + 2 * HDIM)
        sg[:, :, at] = dot(pick, gv[:, at]).astype(BF).reshape(ND, pair, 2 * HDIM)
    sg[:, :, width:] = dot(pick, stat[...].astype(BF)).astype(BF).reshape(ND, pair, HDIM)
    lse = lax.dot_general(pick, l_ref[...], (((1,), (1,)), ((), ())), preferred_element_type=F32)
    sg[:, :, width + heads:width + 2 * heads] = lse.astype(BF).reshape(ND, pair, heads)
    g_copies = exchange(sg, rg_ref, gs, gr)
    for c in g_copies:
        c.start()
    own.append(pltpu.make_async_copy(sg.at[d], rg_ref.at[d], ls.at[3]))
    own[3].start()
    sent = []

    def hop(step, piece):
        cols = pl.ds(piece * kvw, kvw)
        for by, origin, send, recv, half in (
                (1, lax.rem(z - step + NZ, NZ), fs, fr, 0), (NZ - 1, lax.rem(z + step, NZ), bs, br, 1)):
            if step == NZ // 2 - 1 and piece != half:
                continue
            src = mine.at[:, cols] if step == 0 else all_ref.at[origin, :, cols]
            c = along(by, src, all_ref.at[origin, :, cols], send.at[step, piece], recv.at[step, piece])
            c.start()
            sent.append((step, piece, c))

    gather = one_hot_rows(cap, idx_ref[:, :slots])
    for piece, into in enumerate((rk, rv)):
        own[piece].wait()
        for c in kv_copies[piece]:
            c.wait_recv()
        mine[:, piece * kvw:(piece + 1) * kvw] = dot(gather, into[...].reshape(slots, kvw)).astype(BF)
        hop(0, piece)
    own.append(pltpu.make_async_copy(mine, all_ref.at[z], ls.at[4]))
    own[4].start()
    for step in range(1, NZ // 2):
        for piece in range(2):
            for s, p, c in list(sent):
                if s == step - 1 and p == piece:
                    c.wait_recv()
            hop(step, piece)
    for s, p, c in sent:
        if s == NZ // 2 - 1:
            c.wait_recv()
        c.wait_send()
    for c in kv_copies[0] + kv_copies[1]:
        c.wait_send()
    for c in q_copies + g_copies:
        c.wait()
    for c in own[2:]:
        c.wait()


def dispatch(query, keys, values, output, grad_out, log_norm, slot_row, idx_row, cap, pair, cid):
    tok, width = query.shape
    kvw = 2 * keys.shape[1]
    gw = width + HDIM
    dma = pltpu.SemaphoreType.DMA
    return pl.pallas_call(
        dispatch_kernel,
        out_shape=(
            jax.ShapeDtypeStruct((NZ, cap, kvw), BF),
            jax.ShapeDtypeStruct((ND, pair, width), BF),
            jax.ShapeDtypeStruct((ND, pair, gw), BF),
        ),
        in_specs=[ANY_SPEC] * 5 + [VMEM_SPEC] * 3,
        out_specs=(ANY_SPEC,) * 3,
        scratch_shapes=[
            pltpu.VMEM((tok, width), BF), pltpu.VMEM((tok, kvw // 2), BF), pltpu.VMEM((tok, kvw // 2), BF),
            pltpu.VMEM((tok, width), BF), pltpu.VMEM((tok, width), BF), pltpu.VMEM((tok, HDIM), F32),
            pltpu.VMEM((ND, pair, kvw // 2), BF), pltpu.VMEM((ND, pair, kvw // 2), BF),
            pltpu.VMEM((ND, pair, width), BF), pltpu.VMEM((ND, pair, gw), BF),
            pltpu.VMEM((ND, pair, kvw // 2), BF), pltpu.VMEM((ND, pair, kvw // 2), BF), pltpu.VMEM((cap, kvw), BF),
            dma((5,)), dma((ND,)), dma((ND,)), dma((ND,)), dma((ND,)), dma((ND,)), dma((ND,)),
            dma((ND,)), dma((ND,)), dma((5,)),
            dma((4, 2)), dma((4, 2)), dma((4, 2)), dma((4, 2)),
        ],
        compiler_params=pltpu.CompilerParams(
            collective_id=cid, has_side_effects=True, vmem_limit_bytes=56 << 20),
        name="dispatch_rows",
    )(query, keys, values, output, grad_out, log_norm.T, slot_row, idx_row)


def attend_kernel(group, kvh, span_ref, tab_ref, all_hbm, rq_hbm, rg_hbm, row_ref, qpos_ref, dkv_hbm, dq_hbm,
                  all_ref, rq_ref, rg_ref, qs, gs, lse, dlt, dq, dkv, kpos, dkv_ref, dq_ref, probs, dscore, order, ins):
    nq = qs.shape[1]
    capq = nq * QB
    heads = group * kvh
    width = heads * HDIM
    kvw = kvh * HDIM
    scale = HDIM ** -0.5
    cap = all_ref.shape[1]
    tile = NZ * KS
    loads = []
    for n, (src, dst) in enumerate(((rq_hbm, rq_ref), (rg_hbm, rg_ref), (all_hbm, all_ref))):
        c = pltpu.make_async_copy(src, dst, ins.at[n])
        c.start()
        loads.append(c)
    pick = one_hot_rows(capq, row_ref[:, :rq_ref.shape[0]])
    ids = lax.broadcasted_iota(jnp.int32, (cap, HDIM), 0)
    for z in range(NZ):
        p = ids + tab_ref[z, NZ]
        for c in range(NZ):
            jump = tab_ref[z, NZ + c + 1] - tab_ref[z, NZ + c] if c + 1 < NZ else FAR
            p = p + jnp.where(ids >= tab_ref[z, c], jump, 0)
        kpos[z] = p
    dq[...] = jnp.zeros_like(dq)
    dkv[...] = jnp.zeros_like(dkv)
    for load, src, dst in ((loads[0], rq_ref, qs), (loads[1], rg_ref, gs)):
        load.wait()
        for h in range(0, heads, 2):
            both = dot(pick, src[:, h * HDIM:(h + 2) * HDIM]).astype(BF)
            for e in range(2):
                g, r = divmod(h + e, group)
                for i in range(nq):
                    dst[g, i, r * QB:(r + 1) * QB, :] = both[i * QB:(i + 1) * QB, e * HDIM:(e + 1) * HDIM]
    stat = lax.dot_general(rg_ref[:, width:], pick, (((0,), (1,)), ((), ())), preferred_element_type=F32)
    for h in range(heads):
        g, r = divmod(h, group)
        for i in range(nq):
            at = slice(i * QB, (i + 1) * QB)
            to = slice(r * QB, (r + 1) * QB)
            dlt[g, i, :, to] = jnp.broadcast_to(stat[h:h + 1, at], (8, QB))
            lse[g, i, :, to] = jnp.broadcast_to(stat[heads + h:heads + h + 1, at] * LOG2E, (8, QB))
    loads[2].wait()

    def tile_rows(t):
        return pl.ds(pl.multiple_of(t * KS, KS), KS)

    def weigh(n):
        i, slot = order[0, n], n % 2
        rows = tile_rows(order[1, n])
        kp = kpos[:, rows, :].reshape(tile, HDIM)
        seen = (kp <= qpos_ref[i, 0:1, :]) & (kp >= qpos_ref[i, 1:2, :])
        last = (((1,), (1,)), ((), ()))
        for g in range(kvh):
            kt = all_ref[:, rows, g * HDIM:(g + 1) * HDIM].reshape(tile, HDIM)
            vt = all_ref[:, rows, kvw + g * HDIM:kvw + (g + 1) * HDIM].reshape(tile, HDIM)
            s = lax.dot_general(kt, qs[g, i], last, preferred_element_type=F32)
            dp = lax.dot_general(vt, gs[g, i], last, preferred_element_type=F32)
            e = jnp.exp2(s * (scale * LOG2E) - lse[g, i, 0:1, :])
            p = jnp.concatenate(
                [jnp.where(seen, e[:, r * QB:(r + 1) * QB], 0.0) for r in range(group)], axis=1)
            probs[slot, g] = p.astype(BF)
            dscore[slot, g] = (p * (dp - dlt[g, i, 0:1, :]) * scale).astype(BF)

    def add_up(n):
        i, slot = order[0, n], n % 2
        rows = tile_rows(order[1, n])
        for g in range(kvh):
            kc = slice(g * HDIM, (g + 1) * HDIM)
            vc = slice(kvw + g * HDIM, kvw + (g + 1) * HDIM)
            ds = dscore[slot, g]
            dkv[:, rows, vc] += dot(probs[slot, g], gs[g, i]).reshape(NZ, KS, HDIM)
            dkv[:, rows, kc] += dot(ds, qs[g, i]).reshape(NZ, KS, HDIM)
            dq[g, i] += dot_rows(all_ref[:, rows, kc].reshape(tile, HDIM), ds)

    def list_block(i, n):
        def list_tile(t, n):
            order[0, n] = i
            order[1, n] = t
            return n + 1

        return lax.fori_loop(span_ref[0, i], span_ref[1, i], list_tile, n)

    total = lax.fori_loop(0, nq, list_block, jnp.int32(0))

    @pl.when(total > 0)
    def _():
        weigh(0)

    def step(n, _):
        add_up(n)
        weigh(jnp.minimum(n + 1, total))
        return 0

    order[0, total] = 0
    order[1, total] = 0
    lax.fori_loop(0, total, step, 0)
    dkv_ref[...] = dkv[...].astype(BF)
    outs = [pltpu.make_async_copy(dkv_ref, dkv_hbm, ins.at[3])]
    outs[0].start()
    back = pick.T
    for h in range(0, heads, 2):
        cols = []
        for e in range(2):
            g, r = divmod(h + e, group)
            cols.append(jnp.concatenate([dq[g, i, :, r * QB:(r + 1) * QB] for i in range(nq)], axis=1).astype(BF))
        both = lax.dot_general(back, jnp.concatenate(cols, axis=0), (((1,), (1,)), ((), ())),
                               preferred_element_type=F32)
        dq_ref[:, h * HDIM:(h + 2) * HDIM] = both.astype(BF)
    outs.append(pltpu.make_async_copy(dq_ref, dq_hbm, ins.at[4]))
    outs[1].start()
    for c in outs:
        c.wait()


def attend(span, tab, kv_all, rq, rg, idx_row, qpos, group, kvh):
    cap, kvw = kv_all.shape[1:]
    nq = -(-cap // QB)
    slots, width = rq.shape
    return pl.pallas_call(
        functools.partial(attend_kernel, group, kvh),
        out_shape=(
            jax.ShapeDtypeStruct((NZ, cap, kvw), BF),
            jax.ShapeDtypeStruct((slots, width), BF),
        ),
        in_specs=[SMEM_SPEC] * 2 + [ANY_SPEC] * 3 + [VMEM_SPEC] * 2,
        out_specs=(ANY_SPEC, ANY_SPEC),
        scratch_shapes=[
            pltpu.VMEM((NZ, cap, kvw), BF), pltpu.VMEM(rq.shape, BF), pltpu.VMEM(rg.shape, BF),
            pltpu.VMEM((kvh, nq, group * QB, HDIM), BF), pltpu.VMEM((kvh, nq, group * QB, HDIM), BF),
            pltpu.VMEM((kvh, nq, 8, group * QB), F32), pltpu.VMEM((kvh, nq, 8, group * QB), F32),
            pltpu.VMEM((kvh, nq, HDIM, group * QB), F32), pltpu.VMEM((NZ, cap, kvw), F32),
            pltpu.VMEM((NZ, cap, HDIM), jnp.int32),
            pltpu.VMEM((NZ, cap, kvw), BF), pltpu.VMEM((slots, width), BF),
            pltpu.VMEM((2, kvh, NZ * KS, group * QB), BF), pltpu.VMEM((2, kvh, NZ * KS, group * QB), BF),
            pltpu.SMEM((2, nq * (cap // KS) + 1), jnp.int32),
            pltpu.SemaphoreType.DMA((5,)),
        ],
        compiler_params=pltpu.CompilerParams(vmem_limit_bytes=60 << 20),
        name="attention_grads",
    )(span, tab, kv_all, rq, rg, idx_row, qpos)


def return_kernel(dkv_hbm, dq_ref, idx_ref, slot_ref, gq_ref, gk_ref, gv_ref,
                  dkv_ref, fin, bin_, fout, bout, sk, sv, rdq_ref, rk, rv, gq, gk, gv,
                  qs, qr, ks, kr, vs, vr, ls, fs, fr, bs, br):
    z = lax.axis_index("ctx")
    d = lax.axis_index("dp")
    cap, kvw = dkv_ref.shape[1:]
    half_w = kvw // 2
    last = NZ // 2 - 1
    load = pltpu.make_async_copy(dkv_hbm, dkv_ref, ls.at[2])
    load.start()
    greet()
    sent = []

    def hop(step, piece):
        cols = pl.ds(piece * half_w, half_w)
        for by, owner, send, recv, into, out, half in (
                (1, lax.rem(z + NZ // 2 - step, NZ), fs, fr, fin, fout, 0),
                (NZ - 1, lax.rem(z + NZ // 2 + step, NZ), bs, br, bin_, bout, 1)):
            if step == 0 and piece != half:
                continue
            if step == 0 or (step == 1 and piece != half):
                src = dkv_hbm.at[owner, :, cols]
            else:
                for s, p, b, c in sent:
                    if s == step - 1 and p == piece and b == by:
                        c.wait_recv()
                out[step, :, cols] = (dkv_ref[owner, :, cols].astype(F32)
                                      + into[step - 1, :, cols].astype(F32)).astype(BF)
                src = out.at[step, :, cols]
            c = along(by, src, into.at[step, :, cols], send.at[step, piece], recv.at[step, piece])
            c.start()
            sent.append((step, piece, by, c))

    hop(0, 0)
    hop(0, 1)
    dq_copies = exchange(dq_ref, rdq_ref, qs, qr)
    for c in dq_copies:
        c.start()
    own = pltpu.make_async_copy(dq_ref.at[d], rdq_ref.at[d], ls.at[0])
    own.start()
    load.wait()
    for step in range(1, NZ // 2):
        hop(step, 0)
        hop(step, 1)
    own.wait()
    for c in dq_copies:
        c.wait()
    count, width = sk.shape[0] * sk.shape[1], gq.shape[1]
    pick = one_hot_rows(count, slot_ref[...]).T
    rows = rdq_ref[...].reshape(count, width)
    gq[...] = dot(pick, rows).astype(BF)
    outs = [pltpu.make_async_copy(gq, gq_ref, ls.at[3])]
    outs[0].start()
    spread = one_hot_rows(cap, idx_ref[:, :count])
    returns = []
    for piece, (out, into, send, recv) in enumerate(((sk, rk, ks, kr), (sv, rv, vs, vr))):
        cols = slice(piece * half_w, (piece + 1) * half_w)
        for s, p, b, c in sent:
            if s == last and p == piece:
                c.wait_recv()
        total = (dkv_ref[z, :, cols].astype(F32) + fin[last, :, cols].astype(F32)
                 + bin_[last, :, cols].astype(F32)).astype(BF)
        out[...] = dot_rows(spread, total).astype(BF).reshape(out.shape)
        copies = exchange(out, into, send, recv)
        for c in copies:
            c.start()
        keep = pltpu.make_async_copy(out.at[d], into.at[d], ls.at[1 + 3 * piece])
        keep.start()
        returns.append(copies + [keep])
    for s, p, b, c in sent:
        c.wait_send()
    for piece, (into, stage, dst) in enumerate(((rk, gk, gk_ref), (rv, gv, gv_ref))):
        for c in returns[piece]:
            c.wait()
        stage[...] = dot(pick, into[...].reshape(count, half_w)).astype(BF)
        outs.append(pltpu.make_async_copy(stage, dst, ls.at[5 + piece]))
        outs[-1].start()
    for c in outs:
        c.wait()


def send_back(dkv, dq, idx_row, slot_row, cid):
    cap, kvw = dkv.shape[1:]
    pair, width = dq.shape[1:]
    tok = slot_row.shape[1]
    dma = pltpu.SemaphoreType.DMA
    return pl.pallas_call(
        return_kernel,
        out_shape=(
            jax.ShapeDtypeStruct((tok, width), BF),
            jax.ShapeDtypeStruct((tok, kvw // 2), BF),
            jax.ShapeDtypeStruct((tok, kvw // 2), BF),
        ),
        in_specs=[ANY_SPEC, ANY_SPEC, VMEM_SPEC, VMEM_SPEC],
        out_specs=(ANY_SPEC,) * 3,
        scratch_shapes=[pltpu.VMEM((NZ, cap, kvw), BF)] + [pltpu.VMEM((NZ // 2, cap, kvw), BF)] * 4 + [
            pltpu.VMEM((ND, pair, kvw // 2), BF), pltpu.VMEM((ND, pair, kvw // 2), BF),
            pltpu.VMEM((ND, pair, width), BF),
            pltpu.VMEM((ND, pair, kvw // 2), BF), pltpu.VMEM((ND, pair, kvw // 2), BF),
            pltpu.VMEM((tok, width), BF), pltpu.VMEM((tok, kvw // 2), BF), pltpu.VMEM((tok, kvw // 2), BF),
            dma((ND,)), dma((ND,)), dma((ND,)), dma((ND,)), dma((ND,)), dma((ND,)), dma((7,)),
            dma((4, 2)), dma((4, 2)), dma((4, 2)), dma((4, 2)),
        ],
        compiler_params=pltpu.CompilerParams(
            collective_id=cid, has_side_effects=True, vmem_limit_bytes=56 << 20),
        name="return_rows",
    )(dkv, dq, idx_row, slot_row)


def hand_over_kernel(*refs):
    count = (len(refs) - 1) // 2
    sems = refs[-1]
    copies = []
    for n in range(count):
        half = refs[n].shape[0] // 2
        for part in range(2):
            rows = pl.ds(part * half, half)
            copies.append(pltpu.make_async_copy(
                refs[n].at[rows], refs[count + n].at[rows], sems.at[2 * n + part]))
    for c in copies:
        c.start()
    for c in copies:
        c.wait()


def hand_over(arrays):
    return pl.pallas_call(
        hand_over_kernel,
        out_shape=tuple(jax.ShapeDtypeStruct(a.shape, a.dtype) for a in arrays),
        in_specs=[ANY_SPEC] * len(arrays),
        out_specs=(ANY_SPEC,) * len(arrays),
        scratch_shapes=[pltpu.SemaphoreType.DMA((2 * len(arrays),))],
        name="hand_over",
    )(*arrays)


def body(query, keys, values, output, grad_out, log_norm, route_counts, doc_lengths):
    tok = query.shape[0]
    kvh = keys.shape[1] // HDIM
    group = query.shape[1] // keys.shape[1]
    slot, idx, qpos, tab, span, fits = tables(route_counts, doc_lengths, tok)

    def run(size, cid, *rows):
        cap, pair = size
        slots = ND * pair
        kv_all, rq, rg = dispatch(*rows, slot, idx, cap, pair, cid)
        dkv, dq = attend(span, tab, kv_all, rq.reshape(slots, -1), rg.reshape(slots, -1), idx, qpos, group, kvh)
        return hand_over(send_back(dkv, dq.reshape(ND, pair, -1), idx, slot, cid + 1))

    return lax.cond(fits[0] > 0, functools.partial(run, FAST, 0), functools.partial(run, SLOW, 2),
                    query, keys, values, output, grad_out, log_norm)


def solution(mesh):
    rows = P(("ctx", "dp"), "head")
    return jax.shard_map(
        body, mesh=mesh, in_specs=(rows,) * 6 + (P(), P("dp", None)), out_specs=(rows,) * 3, check_vma=False)
```
